256 devices in a mesh: slide: 64 (over z, y, core), grp: 4 (over x).
Axes of the slice: x: 4, y: 4, z: 8, core: 2. Of those that a mesh axis runs over, the one named last changes fastest.
Arguments:
- features: bfloat16 [1024, 131072], P('grp', 'slide'), may hold values from -6 to 6
- tissue: int32 [256, 32], P('slide'), may hold values 0 or 1
- group_owner: int32 [8192, 1], P('slide'), may hold values from 0 to 63; in each aligned block of 128 rows (0 to 127, 128 to 255, ...) at most 4 rows name the same one
- reduce_weight: bfloat16 [256, 1024], P(None, 'grp'), may hold values from -0.1875 to 0.1875
- spatial_weight: bfloat16 [9, 256, 256], P(None, 'grp'), may hold values from -0.125 to 0.125
- expand_weight: bfloat16 [1024, 256], P('grp'), may hold values from -0.375 to 0.375
- reduce_scale: float32 [256], P('grp'), may hold values from 0.25 to 1.75
- reduce_shift: float32 [256], P('grp'), may hold values from -2.5 to 2.5
- spatial_scale: float32 [256], P('grp'), may hold values from 0.25 to 1.75
- spatial_shift: float32 [256], P('grp'), may hold values from -2.5 to 2.5
- expand_scale: float32 [1024], P('grp'), may hold values from 0.25 to 1.75
- expand_shift: float32 [1024], P('grp'), may hold values from -2.5 to 2.5
- upstream: bfloat16 [1024, 131072], P('grp', 'slide'), may hold values from -6 to 6
Outputs:
- merged: bfloat16 [4096, 65536], P('grp', 'slide')
- feature_grad: bfloat16 [1024, 131072], P('grp', 'slide')
- reduce_grad: float32 [256, 1024], P(None, 'grp')
- spatial_grad: float32 [9, 256, 256], P(None, 'grp')
- expand_grad: float32 [1024, 256], P('grp')
The draws below stay inside these ranges and needn't reach their ends.
Inputs may be any that keep to these rules, and one draw needn't show every extreme that they name: `group_owner`: among the 128 tiles of one device, no device is named more than 4 times.
All inputs are finite; a program needn't handle non-finite values. No bound on the sum of `tissue` on one device may be relied on, other than what follows from the above.
Results may differ from the reference program's by a relative error of at most 0.03.
Values may be sent and summed in bfloat16 or wider, within the bound.
No kernel may reach another device: no remote copies, remote signals or barrier semaphores. Data moves between devices by JAX's collectives and lax.ppermute only.
A program may use at most 128 MiB of HBM per device.

```python
import math
import jax
import jax.numpy as jnp
import numpy as np
from jax import lax

C = 1024
M = 256
RR = 4
RC = 32
GRID_C = 8
HR = 16
WR = 128
CELLS = 2048
GROUPS_DEV = 128
CAP2 = 4
N_SLIDE = 64
N_GRP = 4


def place_ends(drawn, stream_key, least, top_value):
    extent = drawn.shape
    spot = [jax.random.randint(jax.random.fold_in(stream_key, axis), (), 0, extent[axis]) for axis in range(len(extent))]
    drawn = drawn.at[tuple(spot)].set(least)
    longest = extent.index(max(extent))
    spot[longest] = (spot[longest] + 1) % extent[longest]
    return drawn.at[tuple(spot)].set(top_value)


def level_of(stream_key, shape, split, low, high):
    def one(position, shards_of):
        heights = jax.random.uniform(jax.random.fold_in(jax.random.fold_in(stream_key, 6), position), (shards_of,), jnp.float32, low / len(split), high / len(split))
        return jnp.repeat(jnp.exp(heights), shape[position] // shards_of).reshape((-1,) + (1,) * (len(shape) - position - 1))

    gain = one(*split[0])
    for cut in split[1:]:
        gain = gain * one(*cut)
    return gain


def shared_out(key, own, number, rows, amount, top, most, lean):
    ranking = jax.random.permutation(key, amount)
    heavy_load, common = shares(amount, rows * top, most, lean, True), shares(amount, rows * top, most, lean, False)
    places = jnp.arange(amount)

    def named(lengths, offset_by):
        used = int((lengths > 0).sum())
        fixed = max(1, used // 4)
        shifted = fixed + (places - fixed + offset_by * (used - fixed)) % max(1, amount - fixed)
        return jnp.zeros((amount,), jnp.int32).at[ranking[jnp.where(places < fixed, places, shifted)]].set(jnp.asarray(lengths, jnp.int32))

    lengths = jnp.where(number % 4 == 0, named(heavy_load, number // 4), named(common, number - number // 4 - 1))
    mixed = jax.random.permutation(jax.random.fold_in(own, 3), amount)
    donor, receiver = mixed[0:amount // 2 * 2:2], mixed[1:amount // 2 * 2:2]
    margin = jnp.minimum(lengths[donor] - 1, most - lengths[receiver]) // 2
    margin = jnp.where((donor == ranking[0]) | (receiver == ranking[0]) | (lengths[receiver] == 0), 0, jnp.maximum(margin, 0))
    shifted = jax.random.randint(jax.random.fold_in(own, 4), (amount // 2,), 0, 1 << 20) % (margin + 1)
    lengths = lengths.at[donor].add(-shifted).at[receiver].add(shifted)
    members = jnp.searchsorted(jnp.cumsum(lengths), jnp.arange(rows * top), side="right").astype(jnp.int32)
    grid = members.reshape(top, rows).T
    grid = grid[jax.random.permutation(jax.random.fold_in(own, 1), rows)]
    offset_by = jax.random.randint(jax.random.fold_in(own, 2), (rows, 1), 0, top)
    return jnp.take_along_axis(grid, (jnp.arange(top)[None, :] + offset_by) % top, axis=1)


def shares(amount, total, limit, slope, full):
    loads = [(1 << 20) // math.isqrt(standing ** slope) + 1 for standing in range(1, amount + 1)]
    largest = limit if full else min(limit, max(-(-total // amount), total * loads[0] // sum(loads)))
    least = 1 if total - largest >= amount - 1 else 0
    counts, spare = [largest] + [least] * (amount - 1), total - largest - least * (amount - 1)
    while spare > 0:
        candidates = [i for i in range(1, amount) if counts[i] < largest] or [i for i in range(1, amount) if counts[i] < limit]
        pool, remaining = sum([loads[i] for i in candidates]), spare
        for i in candidates:
            extra = min(limit - counts[i], max(1, remaining * loads[i] // pool), spare)
            counts[i] = counts[i] + extra
            spare = spare - extra
    return np.array(counts)


def scatter_about(key, shape, spread, bound, split=(), kind=jnp.bfloat16):
    loudness = level_of(key, shape, split, -0.22, 0.18) if split else 1.0
    values = jax.random.normal(key, shape, jnp.float32) * spread * loudness
    return jnp.minimum(jnp.maximum(values, -bound), bound).astype(kind)


def setup_inputs(seed: int = 0) -> dict:
    key_list = jax.random.split(jax.random.key(seed), 14)
    features = scatter_about(key_list[0], (C, N_SLIDE * CELLS), 1.0, 6.0, ((0, 4), (1, 64)))
    tissue = place_ends((jax.random.randint(key_list[1], (N_SLIDE * RR, RC), 0, 4) < 3).astype(jnp.int32), jax.random.fold_in(key_list[1], 1), 0, 1)
    group_owner_keys = jax.random.split(jax.random.fold_in(key_list[2], 1), (N_SLIDE * GROUPS_DEV) // GROUPS_DEV)
    group_owner_turns = jax.random.permutation(jax.random.fold_in(key_list[2], 3), (N_SLIDE * GROUPS_DEV) // GROUPS_DEV)
    group_owner = jax.vmap(lambda own, number: shared_out(jax.random.fold_in(key_list[2], 2), own, number, GROUPS_DEV, N_SLIDE, 1, CAP2, 2))(group_owner_keys, group_owner_turns).reshape((N_SLIDE * GROUPS_DEV, 1))
    reduce_weight = scatter_about(key_list[3], (M, C), C ** -0.5, 0.1875, ((1, 4),))
    spatial_weight = scatter_about(key_list[4], (9, M, M), (9 * M) ** -0.5, 0.125, ((1, 4),))
    expand_weight = scatter_about(key_list[5], (C, M), M ** -0.5, 0.375, ((0, 4),))
    reduce_scale = jnp.clip(1.0 + 0.15 * jax.random.normal(key_list[6], (M,), jnp.float32), 0.25, 1.75)
    reduce_shift = scatter_about(key_list[7], (M,), 0.5, 2.5, ((0, 4),), jnp.float32)
    spatial_scale = jnp.clip(1.0 + 0.15 * jax.random.normal(key_list[8], (M,), jnp.float32), 0.25, 1.75)
    spatial_shift = scatter_about(key_list[9], (M,), 0.5, 2.5, ((0, 4),), jnp.float32)
    expand_scale = jnp.clip(1.0 + 0.15 * jax.random.normal(key_list[10], (C,), jnp.float32), 0.25, 1.75)
    expand_shift = scatter_about(key_list[11], (C,), 0.5, 2.5, ((0, 4),), jnp.float32)
    upstream = scatter_about(key_list[12], (C, N_SLIDE * CELLS), 1.0, 6.0, ((0, 4), (1, 64)))
    return dict(features=features, tissue=tissue, group_owner=group_owner, reduce_weight=reduce_weight, spatial_weight=spatial_weight, expand_weight=expand_weight, reduce_scale=reduce_scale, reduce_shift=reduce_shift, spatial_scale=spatial_scale, spatial_shift=spatial_shift, expand_scale=expand_scale, expand_shift=expand_shift, upstream=upstream)


tap_offsets = ((-1, -1), (-1, 0), (-1, 1), (0, -1), (0, 0), (0, 1), (1, -1), (1, 0), (1, 1))

def gelu_fn(values):
    return jax.nn.gelu(values, approximate=True)

def gelu_back(values, cotangent):
    return jax.vjp(gelu_fn, values)[1](cotangent)[0]

def window_taps(padded, direction, height, breadth):
    pieces = []
    for offset_pair in tap_offsets:
        row_start = 1 + direction * offset_pair[0]
        col_start = 1 + direction * offset_pair[1]
        pieces.append(padded[:, row_start:row_start + height, col_start:col_start + breadth].reshape(padded.shape[0], height * breadth))
    return jnp.stack(pieces, 0)

def rounded_sum(partials):
    running = jnp.zeros(partials[0].shape, jnp.float32)
    for one_term in partials:
        running = running + lax.optimization_barrier(one_term.astype(jnp.bfloat16)).astype(jnp.float32)
    return running

def reference(features, tissue, group_owner, reduce_weight, spatial_weight, expand_weight, reduce_scale, reduce_shift, spatial_scale, spatial_shift, expand_scale, expand_shift, upstream):
    channel_share = C // N_GRP
    mid_share = M // N_GRP
    grid_rows = N_SLIDE // GRID_C
    device_ids = jnp.arange(N_SLIDE, dtype=jnp.int32)
    cell_masks = jnp.repeat(jnp.repeat(tissue.reshape(N_SLIDE, RR, RC), 4, 1), 4, 2).reshape(N_SLIDE, 1, CELLS).astype(jnp.float32)

    def local_columns(array, device_index):
        return lax.dynamic_slice_in_dim(array, device_index * CELLS, CELLS, 1)

    def dense_padded(stacked):
        channels = stacked.shape[1]
        arranged = stacked.reshape(grid_rows, GRID_C, channels, HR, WR).transpose(2, 0, 3, 1, 4)
        return jnp.pad(arranged.reshape(channels, grid_rows * HR, GRID_C * WR), ((0, 0), (1, 1), (1, 1)))

    def window(dense_map, device_index):
        return lax.dynamic_slice(dense_map, (jnp.int32(0), device_index // GRID_C * HR, device_index % GRID_C * WR), (dense_map.shape[0], HR + 2, WR + 2))

    def reduce_block(device_index):
        local_part = local_columns(features, device_index)
        return rounded_sum([jnp.dot(reduce_weight[:, share_index * channel_share:(share_index + 1) * channel_share], local_part[share_index * channel_share:(share_index + 1) * channel_share], preferred_element_type=jnp.float32) for share_index in range(N_GRP)])
    reduced = lax.map(reduce_block, device_ids)
    pre_first = reduce_scale[None, :, None] * reduced + reduce_shift[None, :, None]
    first_act = (cell_masks * gelu_fn(pre_first)).astype(jnp.bfloat16)
    first_map = dense_padded(first_act)
    spatial_float = spatial_weight.astype(jnp.float32)

    def middle_block(device_index):
        mask_here = cell_masks[device_index]
        columns = window_taps(window(first_map, device_index), 1, HR, WR).astype(jnp.float32)
        pre_second = spatial_scale[:, None] * jnp.einsum('toi,tin->on', spatial_float, columns) + spatial_shift[:, None]
        second_act = (mask_here * gelu_fn(pre_second)).astype(jnp.bfloat16)
        expanded = jnp.dot(expand_weight, second_act, preferred_element_type=jnp.float32)
        pre_out = local_columns(features, device_index).astype(jnp.float32) + expand_scale[:, None] * expanded + expand_shift[:, None]
        output = (mask_here * gelu_fn(pre_out)).astype(jnp.bfloat16)
        err_three = gelu_back(pre_out, mask_here * local_columns(upstream, device_index).astype(jnp.float32))
        back_three = (expand_scale[:, None] * err_three).astype(jnp.bfloat16)
        expand_term = jnp.dot(back_three, second_act.T, preferred_element_type=jnp.float32)
        back_second = rounded_sum([jnp.dot(expand_weight[share_index * channel_share:(share_index + 1) * channel_share].T, back_three[share_index * channel_share:(share_index + 1) * channel_share], preferred_element_type=jnp.float32) for share_index in range(N_GRP)])
        err_two = gelu_back(pre_second, mask_here * back_second)
        back_two = (spatial_scale[:, None] * err_two).astype(jnp.bfloat16)
        spatial_term = jnp.einsum('on,tin->toi', back_two.astype(jnp.float32), columns)
        return (output, err_three, back_two, expand_term, spatial_term)
    outputs, err_threes, back_twos, expand_terms, spatial_terms = lax.map(middle_block, device_ids)
    back_map = dense_padded(back_twos)

    def first_back_block(device_index):
        mask_here = cell_masks[device_index]
        back_columns = window_taps(window(back_map, device_index), -1, HR, WR).astype(jnp.float32)
        back_first = rounded_sum([jnp.einsum('toi,ton->in', spatial_float[:, share_index * mid_share:(share_index + 1) * mid_share], back_columns[:, share_index * mid_share:(share_index + 1) * mid_share]) for share_index in range(N_GRP)])
        err_one = gelu_back(pre_first[device_index], mask_here * back_first)
        back_one = (reduce_scale[:, None] * err_one).astype(jnp.bfloat16)
        local_part = local_columns(features, device_index)
        reduce_term = jnp.dot(back_one, local_part.T, preferred_element_type=jnp.float32)
        grad_here = (err_threes[device_index] + jnp.dot(reduce_weight.T, back_one, preferred_element_type=jnp.float32)).astype(jnp.bfloat16)
        return (grad_here, reduce_term)
    grads_stacked, reduce_terms = lax.map(first_back_block, device_ids)
    grad_scale = 1.0 / math.sqrt(N_SLIDE * CELLS)
    reduce_grad = lax.optimization_barrier(jnp.sum(reduce_terms, 0)) * grad_scale
    spatial_grad = lax.optimization_barrier(jnp.sum(spatial_terms, 0)) * grad_scale
    expand_grad = lax.optimization_barrier(jnp.sum(expand_terms, 0)) * grad_scale
    feature_grad = grads_stacked.transpose(1, 0, 2).reshape(C, N_SLIDE * CELLS)
    owners_all = group_owner.reshape(N_SLIDE, GROUPS_DEV)
    owner_hits = (owners_all[:, :, None] == device_ids[None, None, :]).astype(jnp.int32)
    arrival_rank = lax.optimization_barrier(jnp.sum(jnp.cumsum(owner_hits, 1) * owner_hits, 2)) - 1
    slot_index = owners_all * (N_SLIDE * CAP2) + device_ids[:, None] * CAP2 + arrival_rank
    grouped = outputs.reshape(N_SLIDE, C, RR, 2, 2, RC, 2, 2).transpose(1, 4, 7, 0, 2, 5, 3, 6).reshape(4 * C, N_SLIDE * GROUPS_DEV, 4)
    merged = jnp.zeros((4 * C, N_SLIDE * N_SLIDE * CAP2, 4), jnp.bfloat16).at[:, slot_index.reshape(-1), :].set(grouped)
    merged = merged.reshape(4 * C, N_SLIDE * N_SLIDE * CAP2 * 4)
    return (merged, feature_grad, reduce_grad, spatial_grad, expand_grad)
```

```python
import functools
import math

import jax
import jax.numpy as jnp
from jax import lax
from jax.experimental import pallas as pl
from jax.experimental.pallas import tpu as pltpu
from jax.sharding import PartitionSpec as P

F32 = jnp.float32
BF16 = jnp.bfloat16
KAPPA = math.sqrt(2.0 / math.pi)
CUBIC = 0.044715
VMEM_BYTES = 48 * 1024 * 1024

GRID_R = 8
GRID_C = 8
N_SLIDE = 64
N_GRP = 4
TILE_COLS = 32
WIDE = 128
ROWS = 4
OWN = ROWS * WIDE
CELLS = N_GRP * OWN
CH = 256
MID = 256
PARAM_ROWS = 16
TAPS = tuple((a, b) for a in (-1, 0, 1) for b in (-1, 0, 1))
GRAD_SCALE = 1.0 / math.sqrt(N_SLIDE * CELLS)
SP_ROWS = 144
MAT_ROWS = 64


def call(body, outs, *args, flops=0, scratch=(), smem=()):
    spec = pl.BlockSpec(memory_space=pltpu.VMEM)
    scalar = pl.BlockSpec(memory_space=pltpu.SMEM)
    moved = sum(math.prod(s) * jnp.dtype(d).itemsize for s, d in outs)
    moved += sum(math.prod(a.shape) * a.dtype.itemsize for a in args)
    return pl.pallas_call(
        body,
        out_shape=[jax.ShapeDtypeStruct(s, d) for s, d in outs],
        in_specs=[scalar if i in smem else spec for i in range(len(args))],
        out_specs=[spec] * len(outs),
        scratch_shapes=list(scratch),
        compiler_params=pltpu.CompilerParams(vmem_limit_bytes=VMEM_BYTES),
        cost_estimate=pl.CostEstimate(flops=flops, bytes_accessed=moved, transcendentals=0),
    )(*args)


def dot(lhs, rhs, left=1, right=0):
    return lax.dot_general(lhs, rhs, (((left,), (right,)), ((), ())), preferred_element_type=F32)


def act_parts(v):
    sq = v * v
    t = jnp.tanh(KAPPA * (v + CUBIC * (v * sq)))
    half = 0.5 * (1.0 + t)
    slope = half + (0.5 * KAPPA) * v * (1.0 - t * t) * (1.0 + (3.0 * CUBIC) * sq)
    return v * half, slope


def tile_mask(tissue_row):
    spread = (
        lax.broadcasted_iota(jnp.int32, (TILE_COLS, WIDE), 1) // 4
        == lax.broadcasted_iota(jnp.int32, (TILE_COLS, WIDE), 0)
    ).astype(F32)
    row = tissue_row.astype(F32)
    if row.shape[0] == 1:
        row = jnp.broadcast_to(row, (8, TILE_COLS))
    return dot(row, spread)[:1]


def lanes(shape):
    return lax.broadcasted_iota(jnp.int32, shape, len(shape) - 1)


def reduce_kernel(me, feat, weight, params, *outs):
    g = me[0]
    own = lanes((8, MID)) // (MID // N_GRP) == g
    par = jnp.where(own, params[...], 0.0)[:4]
    hi = par.astype(BF16)
    rest = par - hi.astype(F32)
    mid = rest.astype(BF16)
    low = (rest - mid.astype(F32)).astype(BF16)
    tail = jnp.concatenate(
        [hi.astype(F32), mid.astype(F32), low.astype(F32), jnp.zeros((4, MID), F32)], 0
    ).astype(BF16)
    for k in range(N_GRP):
        start = pl.multiple_of(((g + k) % N_GRP) * OWN, OWN)
        block = dot(weight[...], feat[:, pl.ds(start, OWN)])
        outs[k][:MID] = block.astype(BF16)
        outs[k][MID:, :MID] = tail
        outs[k][MID:, MID:] = jnp.zeros((PARAM_ROWS, OWN - MID), BF16)


def first_kernel(me, p0, p1, p2, p3, tissue, act_out, slope_out, cols_out, left_out, right_out):
    g = me[0]
    tails = [p[MID:, :MID].astype(F32) for p in (p0, p1, p2, p3)]
    rows = (tails[0] + tails[1]) + (tails[2] + tails[3])
    par = (rows[0:4] + rows[4:8]) + rows[8:12]
    par = jnp.concatenate([par, jnp.zeros((124, MID), F32)], 0)
    cols = par.T
    cols_out[...] = cols
    mask = tile_mask(tissue[pl.ds(g, 1), :])
    for lo in range(0, MID, 32):
        part = slice(lo, lo + 32)
        scale = cols[part, 0:1]
        shift = cols[part, 1:2]
        lane = lanes((32, WIDE))
        left = jnp.zeros((32, WIDE), F32)
        right = jnp.zeros((32, WIDE), F32)
        for r in range(ROWS):
            seg = slice(r * WIDE, (r + 1) * WIDE)
            total = (p0[part, seg].astype(F32) + p1[part, seg].astype(F32)) + (
                p2[part, seg].astype(F32) + p3[part, seg].astype(F32)
            )
            value, slope = act_parts(scale * total + shift)
            value = mask * value
            act_out[part, seg] = value.astype(BF16)
            slope_out[part, seg] = (scale * mask) * slope
            left = jnp.where(lane == r, value[:, 0:1], left)
            right = jnp.where(lane == r, value[:, WIDE - 1 :], right)
        left_out[part] = left.astype(BF16)
        right_out[part] = right.astype(BF16)


def edge_kernel(grid, left, right, up_out, down_out):
    lane = lanes((MID, WIDE))
    lf = left[...].astype(F32)
    rt = right[...].astype(F32)
    for out, r in ((up_out, 0), (down_out, ROWS - 1)):
        out[:, :WIDE] = grid[:, r * WIDE : (r + 1) * WIDE]
        side = jnp.where(lane == 0, lf[:, r : r + 1], jnp.where(lane == 1, rt[:, r : r + 1], 0.0))
        out[:, WIDE:] = side.astype(BF16)


def shifted(grid, left, right, above, below, out):
    lane = lanes((MID, WIDE))
    lf = left[...].astype(F32)
    rt = right[...].astype(F32)
    ab = above[...].astype(F32)
    be = below[...].astype(F32)
    for r in range(ROWS + 2):
        seg = slice(r * WIDE, (r + 1) * WIDE)
        if r == 0:
            row, lcol, rcol = ab[:, :WIDE], ab[:, WIDE : WIDE + 1], ab[:, WIDE + 1 : WIDE + 2]
        elif r == ROWS + 1:
            row, lcol, rcol = be[:, :WIDE], be[:, WIDE : WIDE + 1], be[:, WIDE + 1 : WIDE + 2]
        else:
            row = grid[:, (r - 1) * WIDE : r * WIDE].astype(F32)
            lcol, rcol = lf[:, r - 1 : r], rt[:, r - 1 : r]
        out[1, :, seg] = row.astype(BF16)
        out[0, :, seg] = jnp.where(lane == 0, lcol, pltpu.roll(row, 1, 1)).astype(BF16)
        out[2, :, seg] = jnp.where(lane == WIDE - 1, rcol, pltpu.roll(row, WIDE - 1, 1)).astype(BF16)


def second_kernel(me, grid, left, right, above, below, weight, cols, tissue, act_out, slope_out, win_out, acc):
    shifted(grid, left, right, above, below, win_out)
    for t, (a, b) in enumerate(TAPS):
        w = jnp.concatenate([weight[q, t] for q in range(N_GRP)], 0)
        start = (a + 1) * WIDE
        part = dot(w, win_out[b + 1, :, start : start + OWN])
        acc[...] = part if t == 0 else acc[...] + part
    mask = tile_mask(tissue[pl.ds(me[0], 1), :])
    for lo in range(0, MID, 32):
        part = slice(lo, lo + 32)
        scale = cols[part, 2:3]
        shift = cols[part, 3:4]
        for r in range(ROWS):
            seg = slice(r * WIDE, (r + 1) * WIDE)
            value, slope = act_parts(scale * acc[part, seg] + shift)
            act_out[part, seg] = (mask * value).astype(BF16)
            slope_out[part, seg] = (scale * mask) * slope


def expand_kernel(me, s0, s1, s2, s3, weight, feat, ups, params, tissue, out, err_out, b0, b1, b2, b3, grad_out, acc, back):
    g = me[0]
    par = jnp.concatenate([params[...], jnp.zeros((120, CH), F32)], 0).T
    grad = None
    for k, (s, b_out) in enumerate(((s0, b0), (s1, b1), (s2, b2), (s3, b3))):
        q = (g + N_GRP - k) % N_GRP
        base = pl.multiple_of(q * OWN, OWN)
        acc[...] = dot(weight[...], s[...])
        mask = tile_mask(tissue[pl.ds(q, 1), :])
        for lo in range(0, CH, 32):
            part = slice(lo, lo + 32)
            scale = par[part, 4:5]
            shift = par[part, 5:6]
            for r in range(ROWS):
                seg = pl.ds(pl.multiple_of(base + r * WIDE, WIDE), WIDE)
                here = slice(r * WIDE, (r + 1) * WIDE)
                pre = feat[part, seg].astype(F32) + scale * acc[part, here] + shift
                value, slope = act_parts(pre)
                err = slope * (mask * ups[part, seg].astype(F32))
                out[part, seg] = (mask * value).astype(BF16)
                err_out[part, seg] = err.astype(BF16)
                back[part, here] = (scale * err).astype(BF16)
        b_out[...] = dot(weight[...], back[...], 0, 0).astype(BF16)
        term = dot(back[...], s[...], 1, 1)
        grad = term if grad is None else grad + term
    put_matrix(grad_out, grad)


def put_matrix(out, matrix):
    for p in range(8):
        h, q = divmod(p, 4)
        out[p] = matrix[q * MAT_ROWS : (q + 1) * MAT_ROWS, h * WIDE : (h + 1) * WIDE].astype(BF16)


def pack_kernel(owner, out, packed):
    col_own = jnp.broadcast_to(owner[...], (WIDE, WIDE))
    sub = lax.broadcasted_iota(jnp.int32, (WIDE, WIDE), 0)
    lane = lanes((WIDE, WIDE))
    row_own = jnp.sum(jnp.where(sub == lane, col_own, 0), 0, keepdims=True)
    rank = jnp.sum(jnp.where((col_own == row_own) & (lane < sub), 1, 0), 1, keepdims=True)
    slot = jnp.broadcast_to(owner[...] * 4 + rank, (WIDE, WIDE))
    pick = lane % 64
    cell = 4 * (pick // 2) + 2 * (pick % 2)
    even = (sub == cell + lane // 64).astype(BF16)
    odd = (sub == cell + 1 - lane // 64).astype(BF16)
    target = []
    for x in range(N_GRP):
        mine = jnp.where(sub == x * TILE_COLS + pick // 2, slot, 0)
        spot = jnp.sum(mine, 0, keepdims=True) * 4 + pick[:1] % 2
        target.append(spot)
    upper = lanes((1, WIDE)) // 64
    low = lanes((CH, WIDE)) < 64
    for j in range(2):
        goal = jnp.concatenate([t + 2 * ((upper + j) % 2) for t in target], 1)
        column = lax.broadcasted_iota(jnp.int32, (4 * CH, OWN), 0)
        select = (column == goal).astype(F32).astype(BF16)
        for i in range(2):
            pieces = []
            for x in range(N_GRP):
                at = x * OWN + i * WIDE
                first = dot(out[:, at : at + WIDE], even)
                second = dot(out[:, at + 2 * WIDE : at + 3 * WIDE], odd)
                if j == 0:
                    pieces.append(jnp.where(low, first, second).astype(BF16))
                else:
                    pieces.append(jnp.where(low, second, first).astype(BF16))
            moved = dot(select, jnp.concatenate(pieces, 1), 1, 1).astype(BF16)
            ij = 2 * i + j
            for h in range(2):
                packed[:, h * 512 + ij * WIDE : h * 512 + (ij + 1) * WIDE] = moved[:, h * WIDE : (h + 1) * WIDE]


def unpack_kernel(packed, out):
    row = lax.broadcasted_iota(jnp.int32, (512, 512), 0)
    col = lanes((512, 512))
    order = (col == (row % 4) * WIDE + row // 4).astype(F32).astype(BF16)
    for h in range(2):
        out[h * 512 : (h + 1) * 512] = dot(order, packed[:, h * 512 : (h + 1) * 512], 1, 1).astype(BF16)


def back_second_kernel(b0, b1, b2, b3, slope, grid_out, left_out, right_out):
    for lo in range(0, MID, 32):
        part = slice(lo, lo + 32)
        lane = lanes((32, WIDE))
        left = jnp.zeros((32, WIDE), F32)
        right = jnp.zeros((32, WIDE), F32)
        for r in range(ROWS):
            seg = slice(r * WIDE, (r + 1) * WIDE)
            total = (b0[part, seg].astype(F32) + b1[part, seg].astype(F32)) + (
                b2[part, seg].astype(F32) + b3[part, seg].astype(F32)
            )
            value = slope[part, seg] * total
            grid_out[part, seg] = value.astype(BF16)
            left = jnp.where(lane == r, value[:, 0:1], left)
            right = jnp.where(lane == r, value[:, WIDE - 1 :], right)
        left_out[part] = left.astype(BF16)
        right_out[part] = right.astype(BF16)


def back_first_kernel(grid, left, right, above, below, weight, slope, back_out, win, acc):
    shifted(grid, left, right, above, below, win)
    for t, (a, b) in enumerate(TAPS):
        w = jnp.concatenate([weight[q, t] for q in range(N_GRP)], 0)
        start = (1 - a) * WIDE
        part = dot(w, win[1 - b, :, start : start + OWN], 0, 0)
        acc[...] = part if t == 0 else acc[...] + part
    back_out[...] = (slope[...] * acc[...]).astype(BF16)


def spatial_kernel(grid, win, expand_part, out):
    for t, (a, b) in enumerate(TAPS):
        start = (a + 1) * WIDE
        term = dot(grid[...], win[b + 1, :, start : start + OWN], 1, 1).astype(BF16)
        for q in range(N_GRP):
            for lo in range(0, 64, 16):
                row = t * 64 + lo
                block, within = divmod(row, SP_ROWS)
                piece = term[q * 64 + lo : q * 64 + lo + 16]
                for h in range(2):
                    at = q * SP_ROWS + within
                    out[h * 4 + block, at : at + 16] = piece[:, h * WIDE : (h + 1) * WIDE]
    out[:, N_GRP * SP_ROWS :] = expand_part[...]


def last_kernel(me, o0, o1, o2, o3, weight, feat, err, out, grad_out):
    g = me[0]
    grad = None
    for k, o in enumerate((o0, o1, o2, o3)):
        base = pl.multiple_of(((g + N_GRP - k) % N_GRP) * OWN, OWN)
        seg = pl.ds(base, OWN)
        out[:, seg] = (err[:, seg].astype(F32) + dot(weight[...], o[...], 0, 0)).astype(BF16)
        term = dot(o[...], feat[:, seg], 1, 1)
        grad = term if grad is None else grad + term
    put_matrix(grad_out, grad)


def early_sum_kernel(me, parts, x0, x1, x2, x3, matrix):
    g = me[0]
    for k, out in enumerate((x0, x1, x2, x3)):
        start = pl.multiple_of(((g + k) % N_GRP) * SP_ROWS, 16)
        total = parts[0, pl.ds(start, SP_ROWS)].astype(F32)
        for p in range(1, 8):
            total = total + parts[p, pl.ds(start, SP_ROWS)].astype(F32)
        out[...] = total.astype(BF16)
    total = parts[0, N_GRP * SP_ROWS :].astype(F32)
    for p in range(1, 8):
        total = total + parts[p, N_GRP * SP_ROWS :].astype(F32)
    matrix[...] = total.astype(BF16)


def plane_sum_kernel(x0, x1, x2, x3, expand_part, parts, out):
    spatial = (x0[...].astype(F32) + x1[...].astype(F32)) + (x2[...].astype(F32) + x3[...].astype(F32))
    total = parts[0].astype(F32)
    for p in range(1, 8):
        total = total + parts[p].astype(F32)
    spatial = spatial.astype(BF16)
    total = total.astype(BF16)
    for p in range(8):
        out[p, :SP_ROWS] = spatial
        out[p, SP_ROWS : SP_ROWS + MAT_ROWS] = expand_part[...]
        out[p, SP_ROWS + MAT_ROWS :] = total


def all_sum_kernel(parts, out):
    total = parts[0].astype(F32)
    for p in range(1, 8):
        total = total + parts[p].astype(F32)
    total = total.astype(BF16)
    for p in range(8):
        out[p] = total


def finish_kernel(parts, reduce_out, spatial_out, expand_out):
    for p in range(8):
        h, q = divmod(p, 4)
        seg = slice(h * WIDE, (h + 1) * WIDE)
        spatial_out[q * SP_ROWS : (q + 1) * SP_ROWS, seg] = parts[p, :SP_ROWS].astype(F32) * GRAD_SCALE
        rows = slice(q * MAT_ROWS, (q + 1) * MAT_ROWS)
        expand_out[rows, seg] = parts[p, SP_ROWS : SP_ROWS + MAT_ROWS].astype(F32) * GRAD_SCALE
        reduce_out[rows, seg] = parts[p, SP_ROWS + MAT_ROWS :].astype(F32) * GRAD_SCALE


def along_grp(block, step):
    return lax.ppermute(block, "grp", [(i, (i + step) % N_GRP) for i in range(N_GRP)])


def column_moves():
    east = []
    for d in range(N_SLIDE):
        if d % GRID_C != GRID_C - 1:
            east.append((d, d + 1))
    return east, [(b, a) for a, b in east]


def row_moves():
    south = []
    for d in range(N_SLIDE):
        for g in range(N_GRP):
            if g < N_GRP - 1:
                south.append((d * N_GRP + g, d * N_GRP + g + 1))
            elif d // GRID_C < GRID_R - 1:
                south.append((d * N_GRP + g, (d + GRID_C) * N_GRP))
    return south, [(b, a) for a, b in south]


def halo(grid, left_strip, right_strip):
    east, west = column_moves()
    south, north = row_moves()
    left = lax.ppermute(right_strip, "slide", east)
    right = lax.ppermute(left_strip, "slide", west)
    up_msg, down_msg = call(edge_kernel, [((MID, 2 * WIDE), BF16)] * 2, grid, left, right)
    above = lax.ppermute(down_msg, ("slide", "grp"), south)
    below = lax.ppermute(up_msg, ("slide", "grp"), north)
    return left, right, above, below


PLANE = [[z * 8 + k for k in range(8)] for z in range(8)]
COLUMN = [[z * 8 + k for z in range(8)] for k in range(8)]


def exchange(pieces, groups):
    return lax.all_to_all(
        pieces, "slide", split_axis=0, concat_axis=0, axis_index_groups=groups, tiled=False
    )


def shards(
    features,
    tissue,
    group_owner,
    reduce_weight,
    spatial_weight,
    expand_weight,
    reduce_scale,
    reduce_shift,
    spatial_scale,
    spatial_shift,
    expand_scale,
    expand_shift,
    upstream,
):
    me = lax.axis_index("grp").astype(jnp.int32).reshape(1)
    own = (MID, OWN)
    weights = lax.all_gather(spatial_weight, "grp", axis=0, tiled=False)
    zero = jnp.zeros((CH,), F32)
    params = jnp.stack(
        [jnp.tile(v, N_GRP) for v in (reduce_scale, reduce_shift, spatial_scale, spatial_shift)]
        + [expand_scale, expand_shift, zero, zero]
    )
    with jax.named_scope("reduce"):
        p = call(
            reduce_kernel,
            [((MID + PARAM_ROWS, OWN), BF16)] * 4,
            me, features, reduce_weight, params,
            smem=(0,), flops=2 * MID * CH * CELLS,
        )
        p = [p[0]] + [along_grp(p[k], k) for k in (1, 2, 3)]
    with jax.named_scope("first"):
        first, slope_one, cols, left, right = call(
            first_kernel,
            [(own, BF16), (own, F32), ((MID, WIDE), F32), ((MID, WIDE), BF16), ((MID, WIDE), BF16)],
            me, *p, tissue,
            smem=(0,), flops=40 * MID * OWN,
        )
        edges = halo(first, left, right)
    with jax.named_scope("second"):
        second, slope_two, win = call(
            second_kernel,
            [(own, BF16), (own, F32), ((3, MID, OWN + 2 * WIDE), BF16)],
            me, first, *edges, weights, cols, tissue,
            smem=(0,), flops=18 * MID * MID * OWN, scratch=[pltpu.VMEM(own, F32)],
        )
        s = [second] + [along_grp(second, k) for k in (1, 2, 3)]
    with jax.named_scope("expand"):
        output, err, b0, b1, b2, b3, expand_part = call(
            expand_kernel,
            [((CH, CELLS), BF16), ((CH, CELLS), BF16)] + [(own, BF16)] * 4 + [((8, MAT_ROWS, WIDE), BF16)],
            me, *s, expand_weight, features, upstream, params, tissue,
            smem=(0,), flops=6 * CH * MID * CELLS,
            scratch=[pltpu.VMEM(own, F32), pltpu.VMEM(own, BF16)],
        )
        b = [b0] + [along_grp(v, -k) for k, v in ((1, b1), (2, b2), (3, b3))]
    with jax.named_scope("merge"):
        packed, = call(
            pack_kernel, [((4 * CH, 4 * CH), BF16)], group_owner, output,
            flops=8 * CH * 4 * CH * OWN,
        )
        arrived = lax.all_to_all(
            packed.reshape(N_SLIDE, 16, 4 * CH), "slide", split_axis=0, concat_axis=0, tiled=False
        ).reshape(4 * CH, 4 * CH)
        merged, = call(
            unpack_kernel, [((4 * CH, 4 * CH), BF16)], arrived, flops=4 * 512 * 512 * 4 * CH,
        )
    with jax.named_scope("back_second"):
        back_two, left, right = call(
            back_second_kernel,
            [(own, BF16), ((MID, WIDE), BF16), ((MID, WIDE), BF16)],
            *b, slope_two, flops=10 * MID * OWN,
        )
        edges = halo(back_two, left, right)
    with jax.named_scope("back_first"):
        back_one, = call(
            back_first_kernel,
            [(own, BF16)],
            back_two, *edges, weights, slope_one,
            flops=18 * MID * MID * OWN,
            scratch=[pltpu.VMEM((3, MID, OWN + 2 * WIDE), BF16), pltpu.VMEM(own, F32)],
        )
        o = [back_one] + [along_grp(back_one, k) for k in (1, 2, 3)]
    with jax.named_scope("spatial"):
        early, = call(
            spatial_kernel,
            [((8, N_GRP * SP_ROWS + MAT_ROWS, WIDE), BF16)],
            back_two, win, expand_part, flops=18 * MID * MID * OWN,
        )
        early = exchange(early, PLANE)
        x0, x1, x2, x3, expand_part = call(
            early_sum_kernel,
            [((SP_ROWS, WIDE), BF16)] * 4 + [((MAT_ROWS, WIDE), BF16)],
            me, early, smem=(0,),
        )
        x = [x0] + [along_grp(v, k) for k, v in ((1, x1), (2, x2), (3, x3))]
    with jax.named_scope("last"):
        feature_grad, reduce_part = call(
            last_kernel,
            [((CH, CELLS), BF16), ((8, MAT_ROWS, WIDE), BF16)],
            me, *o, reduce_weight, features, err,
            smem=(0,), flops=4 * CH * MID * CELLS,
        )
    with jax.named_scope("grads"):
        late = exchange(reduce_part, PLANE)
        height = SP_ROWS + 2 * MAT_ROWS
        plane, = call(plane_sum_kernel, [((8, height, WIDE), BF16)], *x, expand_part, late)
        total, = call(all_sum_kernel, [((8, height, WIDE), BF16)], exchange(plane, COLUMN))
        reduce_grad, spatial_grad, expand_grad = call(
            finish_kernel,
            [((MID, CH), F32), ((9 * 64, MID), F32), ((CH, MID), F32)],
            exchange(total, PLANE),
        )
    return merged, feature_grad, reduce_grad, spatial_grad.reshape(9, 64, MID), expand_grad


def solution(mesh):
    return jax.shard_map(
        shards,
        mesh=mesh,
        in_specs=(
            P("grp", "slide"),
            P("slide", None),
            P("slide", None),
            P(None, "grp"),
            P(None, "grp", None),
            P("grp", None),
            P("grp"),
            P("grp"),
            P("grp"),
            P("grp"),
            P("grp"),
            P("grp"),
            P("grp", "slide"),
        ),
        out_specs=(
            P("grp", "slide"),
            P("grp", "slide"),
            P(None, "grp"),
            P(None, "grp", None),
            P("grp", None),
        ),
        check_vma=False,
    )
```

```python
import functools
import math

import jax
import jax.numpy as jnp
from jax import lax
from jax.experimental import pallas as pl
from jax.experimental.pallas import tpu as pltpu
from jax.sharding import PartitionSpec as P

F32 = jnp.float32
BF16 = jnp.bfloat16
KAPPA = math.sqrt(2.0 / math.pi)
CUBIC = 0.044715
VMEM_BYTES = 48 * 1024 * 1024

GRID_R = 8
GRID_C = 8
N_SLIDE = 64
N_GRP = 4
TILE_COLS = 32
WIDE = 128
ROWS = 4
OWN = ROWS * WIDE
CELLS = N_GRP * OWN
CH = 256
MID = 256
PARAM_ROWS = 16
TAPS = tuple((a, b) for a in (-1, 0, 1) for b in (-1, 0, 1))
GRAD_SCALE = 1.0 / math.sqrt(N_SLIDE * CELLS)
SP_ROWS = 144
MAT_ROWS = 64


def call(body, outs, *args, flops=0, scratch=(), smem=(), after=()):
    spec = pl.BlockSpec()
    scalar = pl.BlockSpec(memory_space=pltpu.SMEM)
    moved = sum(math.prod(s) * jnp.dtype(d).itemsize for s, d in outs)
    moved += sum(math.prod(a.shape) * a.dtype.itemsize for a in args)
    held = len(args)

    def ordered(*refs):
        body(*refs[:held], *refs[held + len(after) :])

    return pl.pallas_call(
        ordered,
        out_shape=[jax.ShapeDtypeStruct(s, d) for s, d in outs],
        in_specs=[scalar if i in smem else spec for i in range(held)]
        + [pl.BlockSpec(memory_space=pl.ANY)] * len(after),
        out_specs=[spec] * len(outs),
        scratch_shapes=list(scratch),
        compiler_params=pltpu.CompilerParams(vmem_limit_bytes=VMEM_BYTES),
        cost_estimate=pl.CostEstimate(flops=flops, bytes_accessed=moved, transcendentals=0),
    )(*args, *after)


def dot(lhs, rhs, left=1, right=0):
    return lax.dot_general(lhs, rhs, (((left,), (right,)), ((), ())), preferred_element_type=F32)


def act_parts(v):
    sq = v * v
    t = jnp.tanh(KAPPA * (v + CUBIC * (v * sq)))
    half = 0.5 * (1.0 + t)
    slope = half + (0.5 * KAPPA) * v * (1.0 - t * t) * (1.0 + (3.0 * CUBIC) * sq)
    return v * half, slope


def tile_mask(tissue_row):
    spread = (
        lax.broadcasted_iota(jnp.int32, (TILE_COLS, WIDE), 1) // 4
        == lax.broadcasted_iota(jnp.int32, (TILE_COLS, WIDE), 0)
    ).astype(F32)
    row = tissue_row.astype(F32)
    if row.shape[0] == 1:
        row = jnp.broadcast_to(row, (8, TILE_COLS))
    return dot(row, spread)[:1]


def lanes(shape):
    return lax.broadcasted_iota(jnp.int32, shape, len(shape) - 1)


def reduce_kernel(me, feat, weight, scales, *outs):
    g = me[0]
    par = jnp.concatenate([scales[...]] * N_GRP, 1)
    par = jnp.where(lanes((4, MID)) // (MID // N_GRP) == g, par, 0.0)
    hi = par.astype(BF16)
    rest = par - hi.astype(F32)
    mid = rest.astype(BF16)
    low = (rest - mid.astype(F32)).astype(BF16)
    tail = jnp.concatenate(
        [hi.astype(F32), mid.astype(F32), low.astype(F32), jnp.zeros((4, MID), F32)], 0
    ).astype(BF16)
    for k in range(N_GRP):
        start = pl.multiple_of(((g + k) % N_GRP) * OWN, OWN)
        block = dot(weight[...], feat[:, pl.ds(start, OWN)])
        outs[k][:MID] = block.astype(BF16)
        outs[k][MID:, :MID] = tail
        outs[k][MID:, MID:] = jnp.zeros((PARAM_ROWS, OWN - MID), BF16)


def first_kernel(me, p0, p1, p2, p3, tissue, act_out, slope_out, cols_out, top_out, bottom_out, left_out, right_out):
    g = me[0]
    tails = [p[MID:, :MID].astype(F32) for p in (p0, p1, p2, p3)]
    rows = (tails[0] + tails[1]) + (tails[2] + tails[3])
    par = (rows[0:4] + rows[4:8]) + rows[8:12]
    par = jnp.concatenate([par, jnp.zeros((124, MID), F32)], 0)
    cols = par.T
    cols_out[...] = cols
    mask = tile_mask(tissue[pl.ds(g, 1), :])
    for lo in range(0, MID, 32):
        part = slice(lo, lo + 32)
        scale = cols[part, 0:1]
        shift = cols[part, 1:2]
        for r in range(ROWS):
            seg = slice(r * WIDE, (r + 1) * WIDE)
            total = (p0[part, seg].astype(F32) + p1[part, seg].astype(F32)) + (
                p2[part, seg].astype(F32) + p3[part, seg].astype(F32)
            )
            value, slope = act_parts(scale * total + shift)
            act_out[part, seg] = (mask * value).astype(BF16)
            slope_out[part, seg] = (scale * mask) * slope
    put_edges(act_out, top_out, bottom_out, left_out, right_out)


def put_edges(grid, top_out, bottom_out, left_out, right_out):
    top_out[...] = grid[:, :WIDE]
    bottom_out[...] = grid[:, (ROWS - 1) * WIDE :]
    lane = lanes((MID, WIDE))
    strip = jnp.zeros((MID, WIDE), F32)
    for r in range(ROWS):
        row = grid[:, r * WIDE : (r + 1) * WIDE].astype(F32)
        strip = jnp.where(lane == r, row[:, 0:1], strip)
        strip = jnp.where(lane == 16 + r, row[:, WIDE - 1 :], strip)
    cells = strip.T
    left_out[...] = cells[:16].astype(BF16)
    right_out[...] = cells[16:32].astype(BF16)


def shifted(me, grid, above, below, west, east, nw, ne, sw, se, out):
    g, s = me[0], me[1]
    north = ((g > 0) | (s >= GRID_C)).astype(F32)
    south = ((g < N_GRP - 1) | (s < N_SLIDE - GRID_C)).astype(F32)
    lhs = (s % GRID_C > 0).astype(F32)
    rhs = (s % GRID_C < GRID_C - 1).astype(F32)
    cells = jnp.concatenate(
        [
            nw[...].astype(F32)[ROWS - 1 : ROWS] * (north * lhs),
            west[...].astype(F32)[:ROWS] * lhs,
            sw[...].astype(F32)[:1] * (south * lhs),
            ne[...].astype(F32)[ROWS - 1 : ROWS] * (north * rhs),
            east[...].astype(F32)[:ROWS] * rhs,
            se[...].astype(F32)[:1] * (south * rhs),
            jnp.zeros((WIDE - 2 * (ROWS + 2), MID), F32),
        ],
        0,
    )
    side = cells.T
    lane = lanes((MID, WIDE))
    for r in range(ROWS + 2):
        seg = slice(r * WIDE, (r + 1) * WIDE)
        if r == 0:
            row = above[...].astype(F32) * north
        elif r == ROWS + 1:
            row = below[...].astype(F32) * south
        else:
            row = grid[:, (r - 1) * WIDE : r * WIDE].astype(F32)
        lcol = side[:, r : r + 1]
        rcol = side[:, ROWS + 2 + r : ROWS + 3 + r]
        out[1, :, seg] = row.astype(BF16)
        out[0, :, seg] = jnp.where(lane == 0, lcol, pltpu.roll(row, 1, 1)).astype(BF16)
        out[2, :, seg] = jnp.where(lane == WIDE - 1, rcol, pltpu.roll(row, WIDE - 1, 1)).astype(BF16)


def second_kernel(me, grid, above, below, west, east, nw, ne, sw, se, weight, cols, tissue, act_out, slope_out, win_out, acc):
    shifted(me, grid, above, below, west, east, nw, ne, sw, se, win_out)
    for t, (a, b) in enumerate(TAPS):
        w = jnp.concatenate([weight[q, t] for q in range(N_GRP)], 0)
        start = (a + 1) * WIDE
        part = dot(w, win_out[b + 1, :, start : start + OWN])
        acc[...] = part if t == 0 else acc[...] + part
    mask = tile_mask(tissue[pl.ds(me[0], 1), :])
    for lo in range(0, MID, 32):
        part = slice(lo, lo + 32)
        scale = cols[part, 2:3]
        shift = cols[part, 3:4]
        for r in range(ROWS):
            seg = slice(r * WIDE, (r + 1) * WIDE)
            value, slope = act_parts(scale * acc[part, seg] + shift)
            act_out[part, seg] = (mask * value).astype(BF16)
            slope_out[part, seg] = (scale * mask) * slope


def expand_kernel(me, s0, s1, s2, s3, weight, feat, ups, scales, shifts, tissue, out, err_out, b0, b1, b2, b3, grad_out, acc, back):
    g = me[0]
    par = jnp.concatenate([scales[...], shifts[...], jnp.zeros((126, CH), F32)], 0).T
    grad = None
    for k, (s, b_out) in enumerate(((s0, b0), (s1, b1), (s2, b2), (s3, b3))):
        q = (g + N_GRP - k) % N_GRP
        base = pl.multiple_of(q * OWN, OWN)
        acc[...] = dot(weight[...], s[...])
        mask = tile_mask(tissue[pl.ds(q, 1), :])
        for lo in range(0, CH, 32):
            part = slice(lo, lo + 32)
            scale = par[part, 0:1]
            shift = par[part, 1:2]
            for r in range(ROWS):
                seg = pl.ds(pl.multiple_of(base + r * WIDE, WIDE), WIDE)
                here = slice(r * WIDE, (r + 1) * WIDE)
                pre = feat[part, seg].astype(F32) + scale * acc[part, here] + shift
                value, slope = act_parts(pre)
                err = slope * (mask * ups[part, seg].astype(F32))
                out[part, seg] = (mask * value).astype(BF16)
                err_out[part, seg] = err.astype(BF16)
                back[part, here] = (scale * err).astype(BF16)
        b_out[...] = dot(weight[...], back[...], 0, 0).astype(BF16)
        term = dot(back[...], s[...], 1, 1)
        grad = term if grad is None else grad + term
    put_matrix(grad_out, grad)


def put_matrix(out, matrix):
    for p in range(8):
        q, h = divmod(p, 2)
        out[p] = matrix[q * MAT_ROWS : (q + 1) * MAT_ROWS, h * WIDE : (h + 1) * WIDE].astype(BF16)


def pack_kernel(owner, out, packed):
    row_own = jnp.broadcast_to(owner[...], (WIDE, WIDE))
    sub = lax.broadcasted_iota(jnp.int32, (WIDE, WIDE), 0)
    lane = lanes((WIDE, WIDE))
    col_own = jnp.sum(jnp.where(sub == lane, row_own, 0), 1, keepdims=True)
    rank = jnp.sum(jnp.where((col_own == row_own) & (lane < sub), 1, 0), 1, keepdims=True)
    slot = jnp.broadcast_to(col_own * 4 + rank, (WIDE, WIDE))
    pick = lane % 64
    cell = 4 * (pick // 2) + 2 * (pick % 2)
    even = (sub == cell + lane // 64).astype(BF16)
    odd = (sub == cell + 1 - lane // 64).astype(BF16)
    target = []
    for x in range(N_GRP):
        mine = jnp.where(sub == x * TILE_COLS + pick // 2, slot, 0)
        spot = jnp.sum(mine, 0, keepdims=True) * 4 + pick[:1] % 2
        target.append(spot)
    upper = lanes((1, WIDE)) // 64
    low = lanes((CH, WIDE)) < 64
    for j in range(2):
        goal = jnp.concatenate([t + 2 * ((upper + j) % 2) for t in target], 1)
        column = lax.broadcasted_iota(jnp.int32, (4 * CH, OWN), 0)
        select = (column == goal).astype(F32).astype(BF16)
        for i in range(2):
            pieces = []
            for x in range(N_GRP):
                at = x * OWN + i * WIDE
                first = dot(out[:, at : at + WIDE], even)
                second = dot(out[:, at + 2 * WIDE : at + 3 * WIDE], odd)
                if j == 0:
                    pieces.append(jnp.where(low, first, second).astype(BF16))
                else:
                    pieces.append(jnp.where(low, second, first).astype(BF16))
            moved = dot(select, jnp.concatenate(pieces, 1), 1, 1).astype(BF16)
            ij = 2 * i + j
            for h in range(2):
                packed[:, h * 512 + ij * WIDE : h * 512 + (ij + 1) * WIDE] = moved[:, h * WIDE : (h + 1) * WIDE]


def unpack_kernel(packed, out):
    row = lax.broadcasted_iota(jnp.int32, (512, 512), 0)
    col = lanes((512, 512))
    order = (col == (row % 4) * WIDE + row // 4).astype(F32).astype(BF16)
    for h in range(2):
        part = slice(h * 512, (h + 1) * 512)
        out[part] = dot(order, packed[:, part], 1, 1).astype(BF16)


def back_second_kernel(b0, b1, b2, b3, slope, grid_out, top_out, bottom_out, left_out, right_out):
    for lo in range(0, MID, 32):
        part = slice(lo, lo + 32)
        total = (b0[part].astype(F32) + b1[part].astype(F32)) + (b2[part].astype(F32) + b3[part].astype(F32))
        grid_out[part] = (slope[part] * total).astype(BF16)
    put_edges(grid_out, top_out, bottom_out, left_out, right_out)


def back_first_kernel(me, grid, above, below, west, east, nw, ne, sw, se, weight, slope, back_out, win, acc):
    shifted(me, grid, above, below, west, east, nw, ne, sw, se, win)
    for t, (a, b) in enumerate(TAPS):
        w = jnp.concatenate([weight[q, t] for q in range(N_GRP)], 0)
        start = (1 - a) * WIDE
        part = dot(w, win[1 - b, :, start : start + OWN], 0, 0)
        acc[...] = part if t == 0 else acc[...] + part
    back_out[...] = (slope[...] * acc[...]).astype(BF16)


def spatial_kernel(me, grid, win, expand_part, keep, send):
    core = me[1] % 2
    for t, (a, b) in enumerate(TAPS):
        start = (a + 1) * WIDE
        term = dot(grid[...], win[b + 1, :, start : start + OWN], 1, 1)
        lo, hi = term[:, :WIDE], term[:, WIDE:]
        mine = jnp.where(core == 0, lo, hi).astype(BF16)
        other = jnp.where(core == 0, hi, lo).astype(BF16)
        for q in range(N_GRP):
            for at in range(0, 64, 16):
                block, within = divmod(t * 64 + at, SP_ROWS)
                rows = slice(q * SP_ROWS + within, q * SP_ROWS + within + 16)
                keep[block, rows] = mine[q * 64 + at : q * 64 + at + 16]
                send[block, rows] = other[q * 64 + at : q * 64 + at + 16]
    for block in range(4):
        keep[block, N_GRP * SP_ROWS :] = expand_part[2 * block + core]
        send[block, N_GRP * SP_ROWS :] = expand_part[2 * block + 1 - core]


def pair_sum_kernel(me, keep, got, y0, y1, y2, y3):
    row = me[1] // 2 % 4
    for k, out in enumerate((y0, y1, y2, y3)):
        q = (row + k) % 4
        out[...] = (keep[q].astype(F32) + got[q].astype(F32)).astype(BF16)


def row_sum_kernel(me, y0, y1, y2, y3, x0, x1, x2, x3, matrix):
    def total(rows):
        return (
            (y0[rows].astype(F32) + y1[rows].astype(F32)) + (y2[rows].astype(F32) + y3[rows].astype(F32))
        ).astype(BF16)

    for k, out in enumerate((x0, x1, x2, x3)):
        start = pl.multiple_of(((me[0] + k) % N_GRP) * SP_ROWS, 16)
        out[...] = total(pl.ds(start, SP_ROWS))
    matrix[...] = total(slice(N_GRP * SP_ROWS, N_GRP * SP_ROWS + MAT_ROWS))


def last_kernel(me, o0, o1, o2, o3, weight, feat, err, out, grad_out, send):
    g = me[0]
    grad = None
    for k, o in enumerate((o0, o1, o2, o3)):
        base = pl.multiple_of(((g + N_GRP - k) % N_GRP) * OWN, OWN)
        seg = pl.ds(base, OWN)
        out[:, seg] = (err[:, seg].astype(F32) + dot(weight[...], o[...], 0, 0)).astype(BF16)
        term = dot(o[...], feat[:, seg], 1, 1)
        grad = term if grad is None else grad + term
    put_matrix(grad_out, grad)
    core = me[1] % 2
    for q in range(4):
        send[q] = grad_out[2 * q + 1 - core]


def total_of(parts):
    total = parts[0].astype(F32)
    for p in range(1, 8):
        total = total + parts[p].astype(F32)
    return total.astype(BF16)


def pair_matrix_kernel(me, part, got, y0, y1, y2, y3):
    core = me[1] % 2
    row = me[1] // 2 % 4
    for k, out in enumerate((y0, y1, y2, y3)):
        q = (row + k) % 4
        out[...] = (part[2 * q + core].astype(F32) + got[q].astype(F32)).astype(BF16)


def plane_sum_kernel(x0, x1, x2, x3, expand_part, y0, y1, y2, y3, out):
    spatial = (x0[...].astype(F32) + x1[...].astype(F32)) + (x2[...].astype(F32) + x3[...].astype(F32))
    total = (y0[...].astype(F32) + y1[...].astype(F32)) + (y2[...].astype(F32) + y3[...].astype(F32))
    spatial = spatial.astype(BF16)
    total = total.astype(BF16)
    for p in range(8):
        out[p, :SP_ROWS] = spatial
        out[p, SP_ROWS : SP_ROWS + MAT_ROWS] = expand_part[...]
        out[p, SP_ROWS + MAT_ROWS :] = total


def all_sum_kernel(parts, out):
    total = total_of(parts)
    for p in range(8):
        out[p] = total


def finish_kernel(parts, reduce_out, spatial_out, expand_out):
    for p in range(8):
        q, h = divmod(p, 2)
        seg = slice(h * WIDE, (h + 1) * WIDE)
        spatial_out[q * SP_ROWS : (q + 1) * SP_ROWS, seg] = parts[p, :SP_ROWS].astype(F32) * GRAD_SCALE
        rows = slice(q * MAT_ROWS, (q + 1) * MAT_ROWS)
        expand_out[rows, seg] = parts[p, SP_ROWS : SP_ROWS + MAT_ROWS].astype(F32) * GRAD_SCALE
        reduce_out[rows, seg] = parts[p, SP_ROWS + MAT_ROWS :].astype(F32) * GRAD_SCALE


def along_grp(block, step):
    return lax.ppermute(block, "grp", [(i, (i + step) % N_GRP) for i in range(N_GRP)])


def pair_swap(block):
    return lax.ppermute(block, "slide", [(d, d ^ 1) for d in range(N_SLIDE)])


def along_row(block, step):
    moves = [(d, d // 8 * 8 + (d + 2 * step) % 8) for d in range(N_SLIDE)]
    return lax.ppermute(block, "slide", moves)


def neighbour(rows, cols):
    moves = []
    for d in range(N_SLIDE):
        for g in range(N_GRP):
            line = (d // GRID_C * N_GRP + g + rows) % (GRID_R * N_GRP)
            there = line // N_GRP * GRID_C + (d % GRID_C + cols) % GRID_C
            moves.append((d * N_GRP + g, there * N_GRP + line % N_GRP))
    return moves


def halo(top, bottom, left, right):
    def to(block, rows, cols):
        return lax.ppermute(block, ("slide", "grp"), neighbour(rows, cols))

    return (
        to(bottom, 1, 0),
        to(top, -1, 0),
        to(right, 0, 1),
        to(left, 0, -1),
        to(right, 1, 1),
        to(left, 1, -1),
        to(right, -1, 1),
        to(left, -1, -1),
    )


PLANE = [[z * 8 + k for k in range(8)] for z in range(8)]
COLUMN = [[z * 8 + k for z in range(8)] for k in range(8)]


def exchange(pieces, groups):
    return lax.all_to_all(
        pieces, "slide", split_axis=0, concat_axis=0, axis_index_groups=groups, tiled=False
    )


def shards(
    features,
    tissue,
    group_owner,
    reduce_weight,
    spatial_weight,
    expand_weight,
    reduce_scale,
    reduce_shift,
    spatial_scale,
    spatial_shift,
    expand_scale,
    expand_shift,
    upstream,
):
    me = jnp.stack([lax.axis_index("grp"), lax.axis_index("slide")]).astype(jnp.int32)
    own = (MID, OWN)
    edge = [((MID, WIDE), BF16)] * 2 + [((16, MID), BF16)] * 2
    weights = lax.all_gather(spatial_weight, "grp", axis=0, tiled=False)
    scales = jnp.stack([reduce_scale, reduce_shift, spatial_scale, spatial_shift])
    with jax.named_scope("reduce"):
        p = call(
            reduce_kernel,
            [((MID + PARAM_ROWS, OWN), BF16)] * 4,
            me, features, reduce_weight, scales,
            smem=(0,), flops=2 * MID * CH * CELLS,
        )
        p = [p[0]] + [along_grp(p[k], k) for k in (1, 2, 3)]
    with jax.named_scope("first"):
        first, slope_one, cols, *edges = call(
            first_kernel,
            [(own, BF16), (own, F32), ((MID, WIDE), F32)] + edge,
            me, *p, tissue,
            smem=(0,), flops=40 * MID * OWN,
        )
        edges = halo(*edges)
    with jax.named_scope("second"):
        second, slope_two, win = call(
            second_kernel,
            [(own, BF16), (own, F32), ((3, MID, OWN + 2 * WIDE), BF16)],
            me, first, *edges, weights, cols, tissue,
            smem=(0,), flops=18 * MID * MID * OWN, scratch=[pltpu.VMEM(own, F32)],
        )
        s = [second] + [along_grp(second, k) for k in (1, 2, 3)]
    with jax.named_scope("expand"):
        output, err, b0, b1, b2, b3, expand_part = call(
            expand_kernel,
            [((CH, CELLS), BF16), ((CH, CELLS), BF16)] + [(own, BF16)] * 4 + [((8, MAT_ROWS, WIDE), BF16)],
            me, *s, expand_weight, features, upstream, expand_scale.reshape(1, -1), expand_shift.reshape(1, -1), tissue,
            smem=(0,), flops=6 * CH * MID * CELLS,
            scratch=[pltpu.VMEM(own, F32), pltpu.VMEM(own, BF16)],
        )
        b = [b0] + [along_grp(v, -k) for k, v in ((1, b1), (2, b2), (3, b3))]
    with jax.named_scope("back_second"):
        back_two, *edges = call(
            back_second_kernel,
            [(own, BF16)] + edge,
            *b, slope_two, flops=10 * MID * OWN,
        )
        edges = halo(*edges)
    with jax.named_scope("spatial"):
        half = (4, N_GRP * SP_ROWS + MAT_ROWS, WIDE)
        keep, send = call(
            spatial_kernel, [(half, BF16)] * 2, me, back_two, win, expand_part,
            smem=(0,), flops=18 * MID * MID * OWN,
        )
        y = call(pair_sum_kernel, [(half[1:], BF16)] * 4, me, keep, pair_swap(send), smem=(0,))
        y = [y[0]] + [along_row(y[k], k) for k in (1, 2, 3)]
        *x, expand_part = call(
            row_sum_kernel, [((SP_ROWS, WIDE), BF16)] * 4 + [((MAT_ROWS, WIDE), BF16)],
            me, *y, smem=(0,),
        )
    with jax.named_scope("back_first"):
        back_one, = call(
            back_first_kernel,
            [(own, BF16)],
            me, back_two, *edges, weights, slope_one,
            smem=(0,), flops=18 * MID * MID * OWN,
            scratch=[pltpu.VMEM((3, MID, OWN + 2 * WIDE), BF16), pltpu.VMEM(own, F32)],
        )
        o = [back_one] + [along_grp(back_one, k) for k in (1, 2, 3)]
    with jax.named_scope("merge"):
        packed, = call(
            pack_kernel, [((4 * CH, 4 * CH), BF16)], group_owner.reshape(1, -1), output,
            flops=8 * CH * 4 * CH * OWN, after=(back_one,),
        )
        arrived = lax.all_to_all(
            packed.reshape(N_SLIDE, 16, 4 * CH), "slide", split_axis=0, concat_axis=0, tiled=False
        ).reshape(4 * CH, 4 * CH)
    with jax.named_scope("early"):
        x = [x[0]] + [along_grp(x[k], k) for k in (1, 2, 3)]
    with jax.named_scope("last"):
        feature_grad, reduce_part, send = call(
            last_kernel,
            [((CH, CELLS), BF16), ((8, MAT_ROWS, WIDE), BF16), ((4, MAT_ROWS, WIDE), BF16)],
            me, *o, reduce_weight, features, err,
            smem=(0,), flops=4 * CH * MID * CELLS, after=(expand_part,),
        )
    with jax.named_scope("merge"):
        merged, = call(
            unpack_kernel, [((4 * CH, 4 * CH), BF16)], arrived,
            flops=4 * 512 * 512 * 4 * CH,
        )
    with jax.named_scope("grads"):
        y = call(
            pair_matrix_kernel, [((MAT_ROWS, WIDE), BF16)] * 4, me, reduce_part, pair_swap(send), smem=(0,)
        )
        y = [y[0]] + [along_row(y[k], k) for k in (1, 2, 3)]
        spread = ((8, SP_ROWS + 2 * MAT_ROWS, WIDE), BF16)
        plane, = call(plane_sum_kernel, [spread], *x, expand_part, *y, after=(arrived,))
        total, = call(all_sum_kernel, [spread], exchange(plane, COLUMN))
        reduce_grad, spatial_grad, expand_grad = call(
            finish_kernel,
            [((MID, CH), F32), ((9 * 64, MID), F32), ((CH, MID), F32)],
            exchange(total, PLANE),
        )
    return merged, feature_grad, reduce_grad, spatial_grad.reshape(9, 64, MID), expand_grad


def solution(mesh):
    return jax.shard_map(
        shards,
        mesh=mesh,
        in_specs=(
            P("grp", "slide"),
            P("slide", None),
            P("slide", None),
            P(None, "grp"),
            P(None, "grp", None),
            P("grp", None),
            P("grp"),
            P("grp"),
            P("grp"),
            P("grp"),
            P("grp"),
            P("grp"),
            P("grp", "slide"),
        ),
        out_specs=(
            P("grp", "slide"),
            P("grp", "slide"),
            P(None, "grp"),
            P(None, "grp", None),
            P("grp", None),
        ),
        check_vma=False,
    )
```

```python
import functools
import math

import jax
import jax.numpy as jnp
from jax import lax
from jax.experimental import pallas as pl
from jax.experimental.pallas import tpu as pltpu
from jax.sharding import PartitionSpec as P

F32 = jnp.float32
BF16 = jnp.bfloat16
KAPPA = math.sqrt(2.0 / math.pi)
CUBIC = 0.044715
VMEM_BYTES = 48 * 1024 * 1024

GRID_R = 8
GRID_C = 8
N_SLIDE = 64
N_GRP = 4
TILE_COLS = 32
WIDE = 128
ROWS = 4
OWN = ROWS * WIDE
CELLS = N_GRP * OWN
CH = 256
MID = 256
PARAM_ROWS = 16
TAPS = tuple((a, b) for a in (-1, 0, 1) for b in (-1, 0, 1))
GRAD_SCALE = 1.0 / math.sqrt(N_SLIDE * CELLS)
SP_ROWS = 144
MAT_ROWS = 64


def call(body, outs, *args, flops=0, scratch=(), smem=(), after=()):
    spec = pl.BlockSpec()
    scalar = pl.BlockSpec(memory_space=pltpu.SMEM)
    moved = sum(math.prod(s) * jnp.dtype(d).itemsize for s, d in outs)
    moved += sum(math.prod(a.shape) * a.dtype.itemsize for a in args)
    held = len(args)

    def ordered(*refs):
        body(*refs[:held], *refs[held + len(after) :])

    return pl.pallas_call(
        ordered,
        out_shape=[jax.ShapeDtypeStruct(s, d) for s, d in outs],
        in_specs=[scalar if i in smem else spec for i in range(held)]
        + [pl.BlockSpec(memory_space=pl.ANY)] * len(after),
        out_specs=[spec] * len(outs),
        scratch_shapes=list(scratch),
        compiler_params=pltpu.CompilerParams(vmem_limit_bytes=VMEM_BYTES),
        cost_estimate=pl.CostEstimate(flops=flops, bytes_accessed=moved, transcendentals=0),
    )(*args, *after)


def dot(lhs, rhs, left=1, right=0):
    return lax.dot_general(lhs, rhs, (((left,), (right,)), ((), ())), preferred_element_type=F32)


def act_parts(v):
    sq = v * v
    t = jnp.tanh(v * (KAPPA + (KAPPA * CUBIC) * sq))
    half = 0.5 + 0.5 * t
    value = v * half
    slope = half + (value * (1.0 - t)) * (KAPPA + (3.0 * KAPPA * CUBIC) * sq)
    return value, slope


def tile_mask(tissue_row):
    spread = (
        lax.broadcasted_iota(jnp.int32, (TILE_COLS, WIDE), 1) // 4
        == lax.broadcasted_iota(jnp.int32, (TILE_COLS, WIDE), 0)
    ).astype(F32)
    row = tissue_row.astype(F32)
    if row.shape[0] == 1:
        row = jnp.broadcast_to(row, (8, TILE_COLS))
    return dot(row, spread)[:1]


def lanes(shape):
    return lax.broadcasted_iota(jnp.int32, shape, len(shape) - 1)


def side_flags(me):
    col = me[1] % GRID_C
    return (col > 0).astype(F32), (col < GRID_C - 1).astype(F32)


def strip_kernel(feat, ups, tissue, left_out, right_out):
    place = lax.broadcasted_iota(jnp.int32, (WIDE, CELLS), 0)
    cell = lanes((WIDE, CELLS))
    kind, row = place % 64 // 16, place % 16
    col = jnp.where(place < 64, kind, WIDE - 1 - kind)
    edge = jnp.where(place < 64, 0, WIDE - 1)
    here = cell // WIDE == row
    pick = (here & (cell % WIDE == col) & (kind < 2)).astype(F32).astype(BF16)
    pick_ups = (here & (cell % WIDE == edge) & (kind == 2)).astype(F32).astype(BF16)
    strips = dot(pick, feat[...], 1, 1) + dot(pick_ups, ups[...], 1, 1)
    tiles = tissue[...].astype(F32)
    for out, lo, at in ((left_out, 0, 0), (right_out, 64, TILE_COLS - 1)):
        out[:48] = strips[lo : lo + 48].astype(BF16)
        flags = [jnp.broadcast_to(tiles[q : q + 1, at : at + 1], (4, CH)) for q in range(N_GRP)]
        out[48:] = jnp.concatenate(flags, 0).astype(BF16)


def reduce_kernel(me, feat, weight, scales, west, east, *outs):
    g = me[0]
    par = jnp.concatenate([scales[...]] * N_GRP, 1)
    par = jnp.where(lanes((4, MID)) // (MID // N_GRP) == g, par, 0.0)
    hi = par.astype(BF16)
    rest = par - hi.astype(F32)
    mid = rest.astype(BF16)
    low = (rest - mid.astype(F32)).astype(BF16)
    tail = jnp.concatenate(
        [hi.astype(F32), mid.astype(F32), low.astype(F32), jnp.zeros((4, MID), F32)], 0
    ).astype(BF16)
    sides = dot(jnp.concatenate([west[:32], east[:32]], 0), weight[...], 1, 1)
    for k in range(N_GRP):
        q = (g + k) % N_GRP
        start = pl.multiple_of(q * OWN, OWN)
        block = dot(weight[...], feat[:, pl.ds(start, OWN)])
        outs[k][:MID] = block.astype(BF16)
        outs[k][MID:, :MID] = tail
        mine = pick_rows(sides, q, 4)
        outs[k][MID:, MID:] = mine.astype(BF16)


def pick_rows(cells, q, groups):
    picked = []
    for n in range(groups):
        rows = jnp.zeros((4, cells.shape[1]), F32)
        for j in range(N_GRP):
            rows = jnp.where(q == j, cells[n * 16 + 4 * j : n * 16 + 4 * j + 4], rows)
        picked.append(rows)
    return jnp.concatenate(picked, 0)


def first_kernel(
    me, p0, p1, p2, p3, tissue, west, east,
    act_out, slope_out, cols_out, rows_out, side_out, side_mask, north_out, south_out,
):
    g = me[0]
    tails = [p[MID:].astype(F32) for p in (p0, p1, p2, p3)]
    rows = (tails[0] + tails[1]) + (tails[2] + tails[3])
    par = (rows[0:4, :MID] + rows[4:8, :MID]) + rows[8:12, :MID]
    rows_out[...] = jnp.concatenate([par, jnp.zeros((4, MID), F32)], 0)
    cols = jnp.concatenate([par, jnp.zeros((124, MID), F32)], 0).T
    cols_out[...] = cols
    lhs, rhs = side_flags(me)
    west_mask = pick_rows(west[48:].astype(F32), g, 1) * lhs
    east_mask = pick_rows(east[48:].astype(F32), g, 1) * rhs
    flags = jnp.concatenate([west_mask, west_mask, east_mask, east_mask], 0)
    side_mask[...] = flags
    side, _ = act_parts(par[0:1] * rows[:, MID:] + par[1:2])
    side_out[...] = (flags * side).astype(BF16)
    mask = tile_mask(tissue[pl.ds(g, 1), :])
    for lo in range(0, MID, 32):
        part = slice(lo, lo + 32)
        scale = cols[part, 0:1]
        shift = cols[part, 1:2]
        for r in range(ROWS):
            seg = slice(r * WIDE, (r + 1) * WIDE)
            total = (p0[part, seg].astype(F32) + p1[part, seg].astype(F32)) + (
                p2[part, seg].astype(F32) + p3[part, seg].astype(F32)
            )
            value, slope = act_parts(scale * total + shift)
            act_out[part, seg] = (mask * value).astype(BF16)
            slope_out[part, seg] = (scale * mask) * slope
    put_edges(act_out, side_out, north_out, south_out)


def put_edges(grid, side, north_out, south_out):
    cells = side[...].astype(F32)
    for out, r in ((north_out, 0), (south_out, ROWS - 1)):
        out[:MID] = grid[:, r * WIDE : (r + 1) * WIDE]
        lines = []
        for n in range(4):
            cell = cells[4 * n + r : 4 * n + r + 1]
            lines += [cell[:, :WIDE], cell[:, WIDE:]]
        out[MID:] = jnp.concatenate(lines + [jnp.zeros((8, WIDE), F32)], 0).astype(BF16)


def side_rows(me, side, above, below):
    g, s = me[0], me[1]
    north = ((g > 0) | (s >= GRID_C)).astype(F32)
    south = ((g < N_GRP - 1) | (s < N_SLIDE - GRID_C)).astype(F32)
    cells = side[...].astype(F32)
    up = above[MID:].astype(F32) * north
    down = below[MID:].astype(F32) * south
    kinds = []
    for n in range(4):
        first = jnp.concatenate([up[2 * n : 2 * n + 1], up[2 * n + 1 : 2 * n + 2]], 1)
        last = jnp.concatenate([down[2 * n : 2 * n + 1], down[2 * n + 1 : 2 * n + 2]], 1)
        kinds.append(jnp.concatenate([first, cells[4 * n : 4 * n + 4], last], 0))
    return north, south, kinds


def shifted(me, grid, side, above, below, out):
    north, south, kinds = side_rows(me, side, above, below)
    columns = jnp.concatenate(
        [kinds[0], kinds[2], jnp.zeros((WIDE - 2 * (ROWS + 2), MID), F32)], 0
    ).T
    lane = lanes((MID, WIDE))
    for r in range(ROWS + 2):
        seg = slice(r * WIDE, (r + 1) * WIDE)
        if r == 0:
            row = above[:MID].astype(F32) * north
        elif r == ROWS + 1:
            row = below[:MID].astype(F32) * south
        else:
            row = grid[:, (r - 1) * WIDE : r * WIDE].astype(F32)
        lcol = columns[:, r : r + 1]
        rcol = columns[:, ROWS + 2 + r : ROWS + 3 + r]
        out[1, :, seg] = row.astype(BF16)
        out[0, :, seg] = jnp.where(lane == 0, lcol, pltpu.roll(row, 1, 1)).astype(BF16)
        out[2, :, seg] = jnp.where(lane == WIDE - 1, rcol, pltpu.roll(row, WIDE - 1, 1)).astype(BF16)
    return kinds


def second_kernel(
    me, grid, side, above, below, weight, cols, rows, side_mask, tissue,
    act_out, slope_out, side_slope, win_out, acc,
):
    near_west, next_west, near_east, next_east = shifted(me, grid, side, above, below, win_out)
    ends = (
        lanes((16, WIDE)) == (WIDE - 1) * (lax.broadcasted_iota(jnp.int32, (16, WIDE), 0) // 8)
    ).astype(F32).astype(BF16)
    firsts, lasts = [], []
    for r in range(ROWS + 2):
        both = dot(ends, win_out[1, :, r * WIDE : (r + 1) * WIDE], 1, 1)
        firsts.append(both[0:1])
        lasts.append(both[8:9])
    first_col = jnp.concatenate(firsts, 0)
    last_col = jnp.concatenate(lasts, 0)
    blank = jnp.zeros((4, MID), F32)
    side_acc = jnp.zeros((16, MID), F32)
    for t, (a, b) in enumerate(TAPS):
        w = jnp.concatenate([weight[q, t] for q in range(N_GRP)], 0)
        start = (a + 1) * WIDE
        part = dot(w, win_out[b + 1, :, start : start + OWN])
        acc[...] = part if t == 0 else acc[...] + part
        lhs = (next_west, near_west, first_col)[b + 1][a + 1 : a + 5]
        rhs = (last_col, near_east, next_east)[b + 1][a + 1 : a + 5]
        patch = jnp.concatenate([lhs, blank, rhs, blank], 0).astype(BF16)
        side_acc = side_acc + dot(patch, w, 1, 1)
    scale_row, shift_row = rows[2:3], rows[3:4]
    value, slope = act_parts(scale_row * side_acc + shift_row)
    act_out[MID:, :MID] = (side_mask[...] * value).astype(BF16)
    act_out[MID:, MID:] = jnp.zeros((16, OWN - MID), BF16)
    side_slope[...] = (scale_row * side_mask[...]) * slope
    mask = tile_mask(tissue[pl.ds(me[0], 1), :])
    for lo in range(0, MID, 32):
        part = slice(lo, lo + 32)
        scale = cols[part, 2:3]
        shift = cols[part, 3:4]
        for r in range(ROWS):
            seg = slice(r * WIDE, (r + 1) * WIDE)
            value, slope = act_parts(scale * acc[part, seg] + shift)
            act_out[part, seg] = (mask * value).astype(BF16)
            slope_out[part, seg] = (scale * mask) * slope


def expand_kernel(me, s0, s1, s2, s3, weight, feat, ups, scales, shifts, tissue, west, east, out, err_out, b0, b1, b2, b3, grad_out, acc, back):
    g = me[0]
    par = jnp.concatenate([scales[...], shifts[...], jnp.zeros((126, CH), F32)], 0).T
    cells = [jnp.zeros((16, MID), F32)] * 2
    group = lax.broadcasted_iota(jnp.int32, (16, MID), 0) // 4
    for k, s in enumerate((s0, s1, s2, s3)):
        q = (g + N_GRP - k) % N_GRP
        tail = s[MID:, :MID].astype(F32)
        for n in range(2):
            cells[n] = jnp.where(group == q, jnp.concatenate([tail[8 * n : 8 * n + 4]] * 4, 0), cells[n])
    scale_row, shift_row = scales[...], shifts[...]
    wide = dot(jnp.concatenate(cells, 0).astype(BF16), weight[...], 1, 1)
    errs = []
    for n, (strip, flag) in enumerate(zip((west, east), side_flags(me))):
        pre = strip[:16].astype(F32) + scale_row * wide[16 * n : 16 * n + 16] + shift_row
        _, slope = act_parts(pre)
        errs.append(scale_row * (slope * (strip[48:].astype(F32) * flag) * strip[32:48].astype(F32)))
    sides = dot(jnp.concatenate(errs, 0).astype(BF16), weight[...])
    blank = jnp.zeros((4, MID), F32)
    grad = None
    for k, (s, b_out) in enumerate(((s0, b0), (s1, b1), (s2, b2), (s3, b3))):
        q = (g + N_GRP - k) % N_GRP
        base = pl.multiple_of(q * OWN, OWN)
        acc[...] = dot(weight[...], s[:MID])
        mine = pick_rows(sides, q, 2)
        b_out[MID:, :MID] = jnp.concatenate([mine[:4], blank, mine[4:], blank], 0).astype(BF16)
        b_out[MID:, MID:] = jnp.zeros((16, OWN - MID), BF16)
        mask = tile_mask(tissue[pl.ds(q, 1), :])
        for lo in range(0, CH, 32):
            part = slice(lo, lo + 32)
            scale = par[part, 0:1]
            shift = par[part, 1:2]
            for r in range(ROWS):
                seg = pl.ds(pl.multiple_of(base + r * WIDE, WIDE), WIDE)
                here = slice(r * WIDE, (r + 1) * WIDE)
                pre = feat[part, seg].astype(F32) + scale * acc[part, here] + shift
                value, slope = act_parts(pre)
                err = slope * (mask * ups[part, seg].astype(F32))
                out[part, seg] = (mask * value).astype(BF16)
                err_out[part, seg] = err.astype(BF16)
                back[part, here] = (scale * err).astype(BF16)
        b_out[:MID] = dot(weight[...], back[...], 0, 0).astype(BF16)
        term = dot(back[...], s[:MID], 1, 1)
        grad = term if grad is None else grad + term
    put_matrix(grad_out, grad)


def put_matrix(out, matrix):
    for p in range(8):
        q, h = divmod(p, 2)
        out[p] = matrix[q * MAT_ROWS : (q + 1) * MAT_ROWS, h * WIDE : (h + 1) * WIDE].astype(BF16)


def pack_kernel(owner, out, packed):
    row_own = jnp.broadcast_to(owner[...], (WIDE, WIDE))
    sub = lax.broadcasted_iota(jnp.int32, (WIDE, WIDE), 0)
    lane = lanes((WIDE, WIDE))
    col_own = jnp.sum(jnp.where(sub == lane, row_own, 0), 1, keepdims=True)
    rank = jnp.sum(jnp.where((col_own == row_own) & (lane < sub), 1, 0), 1, keepdims=True)
    slot = jnp.broadcast_to(col_own * 4 + rank, (WIDE, WIDE))
    pick = lane % 64
    cell = 4 * (pick // 2) + 2 * (pick % 2)
    even = (sub == cell + lane // 64).astype(BF16)
    odd = (sub == cell + 1 - lane // 64).astype(BF16)
    target = []
    for x in range(N_GRP):
        mine = jnp.where(sub == x * TILE_COLS + pick // 2, slot, 0)
        spot = jnp.sum(mine, 0, keepdims=True) * 4 + pick[:1] % 2
        target.append(spot)
    upper = lanes((1, WIDE)) // 64
    low = lanes((CH, WIDE)) < 64
    for j in range(2):
        goal = jnp.concatenate([t + 2 * ((upper + j) % 2) for t in target], 1)
        column = lax.broadcasted_iota(jnp.int32, (4 * CH, OWN), 0)
        select = (column == goal).astype(F32).astype(BF16)
        for i in range(2):
            pieces = []
            for x in range(N_GRP):
                at = x * OWN + i * WIDE
                first = dot(out[:, at : at + WIDE], even)
                second = dot(out[:, at + 2 * WIDE : at + 3 * WIDE], odd)
                if j == 0:
                    pieces.append(jnp.where(low, first, second).astype(BF16))
                else:
                    pieces.append(jnp.where(low, second, first).astype(BF16))
            moved = dot(select, jnp.concatenate(pieces, 1), 1, 1).astype(BF16)
            ij = 2 * i + j
            for h in range(2):
                packed[:, h * 512 + ij * WIDE : h * 512 + (ij + 1) * WIDE] = moved[:, h * WIDE : (h + 1) * WIDE]


def unpack_kernel(packed, out):
    row = lax.broadcasted_iota(jnp.int32, (512, 512), 0)
    col = lanes((512, 512))
    order = (col == (row % 4) * WIDE + row // 4).astype(F32).astype(BF16)
    for h in range(2):
        part = slice(h * 512, (h + 1) * 512)
        out[part] = dot(order, packed[:, part], 1, 1).astype(BF16)


def back_second_kernel(b0, b1, b2, b3, slope, side_slope, grid_out, side_out, north_out, south_out):
    tails = [b[MID:, :MID].astype(F32) for b in (b0, b1, b2, b3)]
    side_out[...] = (side_slope[...] * ((tails[0] + tails[1]) + (tails[2] + tails[3]))).astype(BF16)
    for lo in range(0, MID, 32):
        part = slice(lo, lo + 32)
        total = (b0[part].astype(F32) + b1[part].astype(F32)) + (b2[part].astype(F32) + b3[part].astype(F32))
        grid_out[part] = (slope[part] * total).astype(BF16)
    put_edges(grid_out, side_out, north_out, south_out)


def back_first_kernel(me, grid, side, above, below, weight, slope, back_out, win, acc):
    shifted(me, grid, side, above, below, win)
    for t, (a, b) in enumerate(TAPS):
        w = jnp.concatenate([weight[q, t] for q in range(N_GRP)], 0)
        start = (1 - a) * WIDE
        part = dot(w, win[1 - b, :, start : start + OWN], 0, 0)
        acc[...] = part if t == 0 else acc[...] + part
    back_out[...] = (slope[...] * acc[...]).astype(BF16)


def spatial_kernel(me, grid, win, expand_part, keep, send):
    core = me[1] % 2
    for t, (a, b) in enumerate(TAPS):
        start = (a + 1) * WIDE
        term = dot(grid[...], win[b + 1, :, start : start + OWN], 1, 1)
        lo, hi = term[:, :WIDE], term[:, WIDE:]
        mine = jnp.where(core == 0, lo, hi).astype(BF16)
        other = jnp.where(core == 0, hi, lo).astype(BF16)
        for q in range(N_GRP):
            for at in range(0, 64, 16):
                block, within = divmod(t * 64 + at, SP_ROWS)
                rows = slice(q * SP_ROWS + within, q * SP_ROWS + within + 16)
                keep[block, rows] = mine[q * 64 + at : q * 64 + at + 16]
                send[block, rows] = other[q * 64 + at : q * 64 + at + 16]
    for block in range(4):
        keep[block, N_GRP * SP_ROWS :] = expand_part[2 * block + core]
        send[block, N_GRP * SP_ROWS :] = expand_part[2 * block + 1 - core]


def pair_sum_kernel(me, keep, got, y0, y1, y2, y3):
    row = me[1] // 2 % 4
    for k, out in enumerate((y0, y1, y2, y3)):
        q = (row + k) % 4
        out[...] = (keep[q].astype(F32) + got[q].astype(F32)).astype(BF16)


def row_sum_kernel(me, y0, y1, y2, y3, x0, x1, x2, x3, matrix):
    def total(rows):
        return (
            (y0[rows].astype(F32) + y1[rows].astype(F32)) + (y2[rows].astype(F32) + y3[rows].astype(F32))
        ).astype(BF16)

    for k, out in enumerate((x0, x1, x2, x3)):
        start = pl.multiple_of(((me[0] + k) % N_GRP) * SP_ROWS, 16)
        out[...] = total(pl.ds(start, SP_ROWS))
    matrix[...] = total(slice(N_GRP * SP_ROWS, N_GRP * SP_ROWS + MAT_ROWS))


def last_kernel(me, o0, o1, o2, o3, weight, feat, err, out, grad_out, send):
    g = me[0]
    grad = None
    for k, o in enumerate((o0, o1, o2, o3)):
        base = pl.multiple_of(((g + N_GRP - k) % N_GRP) * OWN, OWN)
        seg = pl.ds(base, OWN)
        out[:, seg] = (err[:, seg].astype(F32) + dot(weight[...], o[...], 0, 0)).astype(BF16)
        term = dot(o[...], feat[:, seg], 1, 1)
        grad = term if grad is None else grad + term
    put_matrix(grad_out, grad)
    core = me[1] % 2
    for q in range(4):
        send[q] = grad_out[2 * q + 1 - core]


def total_of(parts):
    total = parts[0].astype(F32)
    for p in range(1, 8):
        total = total + parts[p].astype(F32)
    return total.astype(BF16)


def pair_matrix_kernel(me, part, got, y0, y1, y2, y3):
    core = me[1] % 2
    row = me[1] // 2 % 4
    for k, out in enumerate((y0, y1, y2, y3)):
        q = (row + k) % 4
        out[...] = (part[2 * q + core].astype(F32) + got[q].astype(F32)).astype(BF16)


def plane_sum_kernel(x0, x1, x2, x3, expand_part, y0, y1, y2, y3, out):
    spatial = (x0[...].astype(F32) + x1[...].astype(F32)) + (x2[...].astype(F32) + x3[...].astype(F32))
    total = (y0[...].astype(F32) + y1[...].astype(F32)) + (y2[...].astype(F32) + y3[...].astype(F32))
    spatial = spatial.astype(BF16)
    total = total.astype(BF16)
    for p in range(8):
        out[p, :SP_ROWS] = spatial
        out[p, SP_ROWS : SP_ROWS + MAT_ROWS] = expand_part[...]
        out[p, SP_ROWS + MAT_ROWS :] = total


def all_sum_kernel(parts, out):
    total = total_of(parts)
    for p in range(8):
        out[p] = total


def finish_kernel(parts, reduce_out, spatial_out, expand_out):
    for p in range(8):
        q, h = divmod(p, 2)
        seg = slice(h * WIDE, (h + 1) * WIDE)
        spatial_out[q * SP_ROWS : (q + 1) * SP_ROWS, seg] = parts[p, :SP_ROWS].astype(F32) * GRAD_SCALE
        rows = slice(q * MAT_ROWS, (q + 1) * MAT_ROWS)
        expand_out[rows, seg] = parts[p, SP_ROWS : SP_ROWS + MAT_ROWS].astype(F32) * GRAD_SCALE
        reduce_out[rows, seg] = parts[p, SP_ROWS + MAT_ROWS :].astype(F32) * GRAD_SCALE


def along_grp(block, step):
    return lax.ppermute(block, "grp", [(i, (i + step) % N_GRP) for i in range(N_GRP)])


def pair_swap(block):
    return lax.ppermute(block, "slide", [(d, d ^ 1) for d in range(N_SLIDE)])


def along_row(block, step):
    moves = [(d, d // 8 * 8 + (d + 2 * step) % 8) for d in range(N_SLIDE)]
    return lax.ppermute(block, "slide", moves)


def beside(block, step):
    moves = [(d, d // GRID_C * GRID_C + (d + step) % GRID_C) for d in range(N_SLIDE)]
    return lax.ppermute(block, "slide", moves)


def line_moves(step):
    moves = []
    for d in range(N_SLIDE):
        for g in range(N_GRP):
            line = (d // GRID_C * N_GRP + g + step) % (GRID_R * N_GRP)
            there = line // N_GRP * GRID_C + d % GRID_C
            moves.append((d * N_GRP + g, there * N_GRP + line % N_GRP))
    return moves


def halo(north, south):
    above = lax.ppermute(south, ("slide", "grp"), line_moves(1))
    below = lax.ppermute(north, ("slide", "grp"), line_moves(-1))
    return above, below


PLANE = [[z * 8 + k for k in range(8)] for z in range(8)]
COLUMN = [[z * 8 + k for z in range(8)] for k in range(8)]


def exchange(pieces, groups):
    return lax.all_to_all(
        pieces, "slide", split_axis=0, concat_axis=0, axis_index_groups=groups, tiled=False
    )


def shards(
    features,
    tissue,
    group_owner,
    reduce_weight,
    spatial_weight,
    expand_weight,
    reduce_scale,
    reduce_shift,
    spatial_scale,
    spatial_shift,
    expand_scale,
    expand_shift,
    upstream,
):
    me = jnp.stack([lax.axis_index("grp"), lax.axis_index("slide")]).astype(jnp.int32)
    own = (MID, OWN)
    long = (MID + PARAM_ROWS, OWN)
    side = (16, MID)
    edge = [((MID + 16, WIDE), BF16)] * 2
    strips = call(strip_kernel, [((64, CH), BF16)] * 2, features, upstream, tissue, flops=4 * WIDE * CH * CELLS)
    east, west = beside(strips[0], -1), beside(strips[1], 1)
    weights = lax.all_gather(spatial_weight, "grp", axis=0, tiled=False)
    scales = jnp.stack([reduce_scale, reduce_shift, spatial_scale, spatial_shift])
    with jax.named_scope("reduce"):
        p = call(
            reduce_kernel,
            [(long, BF16)] * 4,
            me, features, reduce_weight, scales, west, east,
            smem=(0,), flops=2 * MID * CH * CELLS,
        )
        p = [p[0]] + [along_grp(p[k], k) for k in (1, 2, 3)]
    with jax.named_scope("first"):
        first, slope_one, cols, rows, side_one, side_mask, *edges = call(
            first_kernel,
            [(own, BF16), (own, F32), ((MID, WIDE), F32), ((8, MID), F32), (side, BF16), (side, F32)] + edge,
            me, *p, tissue, west, east,
            smem=(0,), flops=40 * MID * OWN,
        )
        edges = halo(*edges)
    with jax.named_scope("second"):
        second, slope_two, side_slope, win = call(
            second_kernel,
            [(long, BF16), (own, F32), (side, F32), ((3, MID, OWN + 2 * WIDE), BF16)],
            me, first, side_one, *edges, weights, cols, rows, side_mask, tissue,
            smem=(0,), flops=18 * MID * MID * OWN, scratch=[pltpu.VMEM(own, F32)],
        )
        s = [second] + [along_grp(second, k) for k in (1, 2, 3)]
    with jax.named_scope("expand"):
        output, err, b0, b1, b2, b3, expand_part = call(
            expand_kernel,
            [((CH, CELLS), BF16), ((CH, CELLS), BF16)] + [(long, BF16)] * 4 + [((8, MAT_ROWS, WIDE), BF16)],
            me, *s, expand_weight, features, upstream, expand_scale.reshape(1, -1), expand_shift.reshape(1, -1), tissue, west, east,
            smem=(0,), flops=6 * CH * MID * CELLS,
            scratch=[pltpu.VMEM(own, F32), pltpu.VMEM(own, BF16)],
        )
        b = [b0] + [along_grp(v, -k) for k, v in ((1, b1), (2, b2), (3, b3))]
    with jax.named_scope("back_second"):
        back_two, side_two, *edges = call(
            back_second_kernel,
            [(own, BF16), (side, BF16)] + edge,
            *b, slope_two, side_slope, flops=10 * MID * OWN,
        )
        edges = halo(*edges)
    with jax.named_scope("spatial"):
        half = (4, N_GRP * SP_ROWS + MAT_ROWS, WIDE)
        keep, send = call(
            spatial_kernel, [(half, BF16)] * 2, me, back_two, win, expand_part,
            smem=(0,), flops=18 * MID * MID * OWN,
        )
        y = call(pair_sum_kernel, [(half[1:], BF16)] * 4, me, keep, pair_swap(send), smem=(0,))
        y = [y[0]] + [along_row(y[k], k) for k in (1, 2, 3)]
        *x, expand_part = call(
            row_sum_kernel, [((SP_ROWS, WIDE), BF16)] * 4 + [((MAT_ROWS, WIDE), BF16)],
            me, *y, smem=(0,),
        )
    with jax.named_scope("back_first"):
        back_one, = call(
            back_first_kernel,
            [(own, BF16)],
            me, back_two, side_two, *edges, weights, slope_one,
            smem=(0,), flops=18 * MID * MID * OWN,
            scratch=[pltpu.VMEM((3, MID, OWN + 2 * WIDE), BF16), pltpu.VMEM(own, F32)],
        )
        o = [back_one] + [along_grp(back_one, k) for k in (1, 2, 3)]
    with jax.named_scope("merge"):
        packed, = call(
            pack_kernel, [((4 * CH, 4 * CH), BF16)], group_owner.reshape(1, -1), output,
            flops=8 * CH * 4 * CH * OWN, after=(back_one,),
        )
        arrived = lax.all_to_all(
            packed.reshape(N_SLIDE, 16, 4 * CH), "slide", split_axis=0, concat_axis=0, tiled=False
        ).reshape(4 * CH, 4 * CH)
    with jax.named_scope("early"):
        x = [x[0]] + [along_grp(x[k], k) for k in (1, 2, 3)]
    with jax.named_scope("last"):
        feature_grad, reduce_part, send = call(
            last_kernel,
            [((CH, CELLS), BF16), ((8, MAT_ROWS, WIDE), BF16), ((4, MAT_ROWS, WIDE), BF16)],
            me, *o, reduce_weight, features, err,
            smem=(0,), flops=4 * CH * MID * CELLS, after=(expand_part,),
        )
    with jax.named_scope("merge"):
        merged, = call(
            unpack_kernel, [((4 * CH, 4 * CH), BF16)], arrived,
            flops=4 * 512 * 512 * 4 * CH,
        )
    with jax.named_scope("grads"):
        y = call(
            pair_matrix_kernel, [((MAT_ROWS, WIDE), BF16)] * 4, me, reduce_part, pair_swap(send), smem=(0,)
        )
        y = [y[0]] + [along_row(y[k], k) for k in (1, 2, 3)]
        spread = ((8, SP_ROWS + 2 * MAT_ROWS, WIDE), BF16)
        plane, = call(plane_sum_kernel, [spread], *x, expand_part, *y, after=(arrived,))
        total, = call(all_sum_kernel, [spread], exchange(plane, COLUMN))
        reduce_grad, spatial_grad, expand_grad = call(
            finish_kernel,
            [((MID, CH), F32), ((9 * 64, MID), F32), ((CH, MID), F32)],
            exchange(total, PLANE),
        )
    return merged, feature_grad, reduce_grad, spatial_grad.reshape(9, 64, MID), expand_grad


def solution(mesh):
    return jax.shard_map(
        shards,
        mesh=mesh,
        in_specs=(
            P("grp", "slide"),
            P("slide", None),
            P("slide", None),
            P(None, "grp"),
            P(None, "grp", None),
            P("grp", None),
            P("grp"),
            P("grp"),
            P("grp"),
            P("grp"),
            P("grp"),
            P("grp"),
            P("grp", "slide"),
        ),
        out_specs=(
            P("grp", "slide"),
            P("grp", "slide"),
            P(None, "grp"),
            P(None, "grp", None),
            P("grp", None),
        ),
        check_vma=False,
    )
```

```python
import functools
import math

import jax
import jax.numpy as jnp
from jax import lax
from jax.experimental import pallas as pl
from jax.experimental.pallas import tpu as pltpu
from jax.sharding import PartitionSpec as P

F32 = jnp.float32
BF16 = jnp.bfloat16
KAPPA = math.sqrt(2.0 / math.pi)
CUBIC = 0.044715
VMEM_BYTES = 48 * 1024 * 1024

GRID_R = 8
GRID_C = 8
N_SLIDE = 64
N_GRP = 4
TILE_COLS = 32
WIDE = 128
ROWS = 4
OWN = ROWS * WIDE
CELLS = N_GRP * OWN
CH = 256
MID = 256
PARAM_ROWS = 16
TAPS = tuple((a, b) for a in (-1, 0, 1) for b in (-1, 0, 1))
GRAD_SCALE = 1.0 / math.sqrt(N_SLIDE * CELLS)
SP_ROWS = 144
MAT_ROWS = 64


def call(body, outs, *args, flops=0, scratch=(), smem=(), after=()):
    spec = pl.BlockSpec()
    scalar = pl.BlockSpec(memory_space=pltpu.SMEM)
    moved = sum(math.prod(s) * jnp.dtype(d).itemsize for s, d in outs)
    moved += sum(math.prod(a.shape) * a.dtype.itemsize for a in args)
    held = len(args)

    def ordered(*refs):
        body(*refs[:held], *refs[held + len(after) :])

    return pl.pallas_call(
        ordered,
        out_shape=[jax.ShapeDtypeStruct(s, d) for s, d in outs],
        in_specs=[scalar if i in smem else spec for i in range(held)]
        + [pl.BlockSpec(memory_space=pl.ANY)] * len(after),
        out_specs=[spec] * len(outs),
        scratch_shapes=list(scratch),
        compiler_params=pltpu.CompilerParams(vmem_limit_bytes=VMEM_BYTES),
        cost_estimate=pl.CostEstimate(flops=flops, bytes_accessed=moved, transcendentals=0),
    )(*args, *after)


def gate(array, *after):
    place = pl.BlockSpec(memory_space=pl.ANY)
    return pl.pallas_call(
        lambda *refs: None,
        out_shape=jax.ShapeDtypeStruct(array.shape, array.dtype),
        in_specs=[place] * (1 + len(after)),
        out_specs=place,
        input_output_aliases={0: 0},
    )(array, *after)


def dot(lhs, rhs, left=1, right=0):
    return lax.dot_general(lhs, rhs, (((left,), (right,)), ((), ())), preferred_element_type=F32)


def act_parts(v):
    sq = v * v
    t = jnp.tanh(v * (KAPPA + (KAPPA * CUBIC) * sq))
    half = 0.5 + 0.5 * t
    value = v * half
    slope = half + (value * (1.0 - t)) * (KAPPA + (3.0 * KAPPA * CUBIC) * sq)
    return value, slope


def tile_mask(tissue_row):
    spread = (
        lax.broadcasted_iota(jnp.int32, (TILE_COLS, WIDE), 1) // 4
        == lax.broadcasted_iota(jnp.int32, (TILE_COLS, WIDE), 0)
    ).astype(F32)
    row = tissue_row.astype(F32)
    if row.shape[0] == 1:
        row = jnp.broadcast_to(row, (8, TILE_COLS))
    return dot(row, spread)[:1]


def lanes(shape):
    return lax.broadcasted_iota(jnp.int32, shape, len(shape) - 1)


def side_flags(me):
    col = me[1] % GRID_C
    return (col > 0).astype(F32), (col < GRID_C - 1).astype(F32)


def strip_kernel(feat, ups, tissue, left_out, right_out):
    place = lax.broadcasted_iota(jnp.int32, (WIDE, CELLS), 0)
    cell = lanes((WIDE, CELLS))
    kind, row = place % 64 // 16, place % 16
    col = jnp.where(place < 64, kind, WIDE - 1 - kind)
    edge = jnp.where(place < 64, 0, WIDE - 1)
    here = cell // WIDE == row
    pick = (here & (cell % WIDE == col) & (kind < 2)).astype(F32).astype(BF16)
    pick_ups = (here & (cell % WIDE == edge) & (kind == 2)).astype(F32).astype(BF16)
    strips = dot(pick, feat[...], 1, 1) + dot(pick_ups, ups[...], 1, 1)
    tiles = tissue[...].astype(F32)
    for out, lo, at in ((left_out, 0, 0), (right_out, 64, TILE_COLS - 1)):
        out[:48] = strips[lo : lo + 48].astype(BF16)
        flags = [jnp.broadcast_to(tiles[q : q + 1, at : at + 1], (4, CH)) for q in range(N_GRP)]
        out[48:] = jnp.concatenate(flags, 0).astype(BF16)


def reduce_kernel(me, feat, weight, scales, west, east, *outs):
    g = me[0]
    par = jnp.concatenate([scales[...]] * N_GRP, 1)
    par = jnp.where(lanes((4, MID)) // (MID // N_GRP) == g, par, 0.0)
    hi = par.astype(BF16)
    rest = par - hi.astype(F32)
    mid = rest.astype(BF16)
    low = (rest - mid.astype(F32)).astype(BF16)
    tail = jnp.concatenate(
        [hi.astype(F32), mid.astype(F32), low.astype(F32), jnp.zeros((4, MID), F32)], 0
    ).astype(BF16)
    sides = dot(jnp.concatenate([west[:32], east[:32]], 0), weight[...], 1, 1)
    for k in range(N_GRP):
        q = (g + k) % N_GRP
        start = pl.multiple_of(q * OWN, OWN)
        block = dot(weight[...], feat[:, pl.ds(start, OWN)])
        outs[k][:MID] = block.astype(BF16)
        outs[k][MID:, :MID] = tail
        mine = pick_rows(sides, q, 4)
        outs[k][MID:, MID:] = mine.astype(BF16)


def pick_rows(cells, q, groups):
    picked = []
    for n in range(groups):
        rows = jnp.zeros((4, cells.shape[1]), F32)
        for j in range(N_GRP):
            rows = jnp.where(q == j, cells[n * 16 + 4 * j : n * 16 + 4 * j + 4], rows)
        picked.append(rows)
    return jnp.concatenate(picked, 0)


def weights_kernel(me, w0, w1, w2, w3, out):
    for k, w in enumerate((w0, w1, w2, w3)):
        out[(me[0] + N_GRP - k) % N_GRP] = w[...]


def tap_weight(me, mine, other, t):
    core = me[1] % 2
    rows = []
    for q in range(N_GRP):
        here, there = mine[q, t], other[q, t]
        rows += [jnp.where(core == 0, here, there), jnp.where(core == 0, there, here)]
    return jnp.concatenate(rows, 0)


def first_kernel(
    me, p0, p1, p2, p3, tissue, west, east,
    act_out, slope_out, cols_out, rows_out, side_out, side_mask, north_out, south_out,
):
    g = me[0]
    tails = [p[MID:].astype(F32) for p in (p0, p1, p2, p3)]
    rows = (tails[0] + tails[1]) + (tails[2] + tails[3])
    par = (rows[0:4, :MID] + rows[4:8, :MID]) + rows[8:12, :MID]
    rows_out[...] = jnp.concatenate([par, jnp.zeros((4, MID), F32)], 0)
    cols = jnp.concatenate([par, jnp.zeros((124, MID), F32)], 0).T
    cols_out[...] = cols
    lhs, rhs = side_flags(me)
    west_mask = pick_rows(west[48:].astype(F32), g, 1) * lhs
    east_mask = pick_rows(east[48:].astype(F32), g, 1) * rhs
    flags = jnp.concatenate([west_mask, west_mask, east_mask, east_mask], 0)
    side_mask[...] = flags
    side, _ = act_parts(par[0:1] * rows[:, MID:] + par[1:2])
    side_out[...] = (flags * side).astype(BF16)
    mask = tile_mask(tissue[pl.ds(g, 1), :])
    for lo in range(0, MID, 32):
        part = slice(lo, lo + 32)
        scale = cols[part, 0:1]
        shift = cols[part, 1:2]
        for r in range(ROWS):
            seg = slice(r * WIDE, (r + 1) * WIDE)
            total = (p0[part, seg].astype(F32) + p1[part, seg].astype(F32)) + (
                p2[part, seg].astype(F32) + p3[part, seg].astype(F32)
            )
            value, slope = act_parts(scale * total + shift)
            act_out[part, seg] = (mask * value).astype(BF16)
            slope_out[part, seg] = (scale * mask) * slope
    put_edges(act_out, side_out, north_out, south_out)


def put_edges(grid, side, north_out, south_out):
    cells = side[...].astype(F32)
    for out, r in ((north_out, 0), (south_out, ROWS - 1)):
        out[:MID] = grid[:, r * WIDE : (r + 1) * WIDE]
        lines = []
        for n in range(4):
            cell = cells[4 * n + r : 4 * n + r + 1]
            lines += [cell[:, :WIDE], cell[:, WIDE:]]
        out[MID:] = jnp.concatenate(lines + [jnp.zeros((8, WIDE), F32)], 0).astype(BF16)


def side_rows(me, side, above, below):
    g, s = me[0], me[1]
    north = ((g > 0) | (s >= GRID_C)).astype(F32)
    south = ((g < N_GRP - 1) | (s < N_SLIDE - GRID_C)).astype(F32)
    cells = side[...].astype(F32)
    up = above[MID:].astype(F32) * north
    down = below[MID:].astype(F32) * south
    kinds = []
    for n in range(4):
        first = jnp.concatenate([up[2 * n : 2 * n + 1], up[2 * n + 1 : 2 * n + 2]], 1)
        last = jnp.concatenate([down[2 * n : 2 * n + 1], down[2 * n + 1 : 2 * n + 2]], 1)
        kinds.append(jnp.concatenate([first, cells[4 * n : 4 * n + 4], last], 0))
    return north, south, kinds


def shifted(me, grid, side, above, below, out):
    north, south, kinds = side_rows(me, side, above, below)
    columns = jnp.concatenate(
        [kinds[0], kinds[2], jnp.zeros((WIDE - 2 * (ROWS + 2), MID), F32)], 0
    ).T
    lane = lanes((MID, WIDE))
    for r in range(ROWS + 2):
        seg = slice(r * WIDE, (r + 1) * WIDE)
        if r == 0:
            row = above[:MID].astype(F32) * north
        elif r == ROWS + 1:
            row = below[:MID].astype(F32) * south
        else:
            row = grid[:, (r - 1) * WIDE : r * WIDE].astype(F32)
        lcol = columns[:, r : r + 1]
        rcol = columns[:, ROWS + 2 + r : ROWS + 3 + r]
        out[1, :, seg] = row.astype(BF16)
        out[0, :, seg] = jnp.where(lane == 0, lcol, pltpu.roll(row, 1, 1)).astype(BF16)
        out[2, :, seg] = jnp.where(lane == WIDE - 1, rcol, pltpu.roll(row, WIDE - 1, 1)).astype(BF16)
    return kinds


def second_kernel(
    me, grid, side, above, below, mine, other, cols, rows, side_mask, tissue,
    act_out, slope_out, side_slope, win_out, acc,
):
    near_west, next_west, near_east, next_east = shifted(me, grid, side, above, below, win_out)
    ends = (
        lanes((16, WIDE)) == (WIDE - 1) * (lax.broadcasted_iota(jnp.int32, (16, WIDE), 0) // 8)
    ).astype(F32).astype(BF16)
    firsts, lasts = [], []
    for r in range(ROWS + 2):
        both = dot(ends, win_out[1, :, r * WIDE : (r + 1) * WIDE], 1, 1)
        firsts.append(both[0:1])
        lasts.append(both[8:9])
    first_col = jnp.concatenate(firsts, 0)
    last_col = jnp.concatenate(lasts, 0)
    blank = jnp.zeros((4, MID), F32)
    side_acc = jnp.zeros((16, MID), F32)
    for t, (a, b) in enumerate(TAPS):
        w = tap_weight(me, mine, other, t)
        start = (a + 1) * WIDE
        part = dot(w, win_out[b + 1, :, start : start + OWN])
        acc[...] = part if t == 0 else acc[...] + part
        lhs = (next_west, near_west, first_col)[b + 1][a + 1 : a + 5]
        rhs = (last_col, near_east, next_east)[b + 1][a + 1 : a + 5]
        patch = jnp.concatenate([lhs, blank, rhs, blank], 0).astype(BF16)
        side_acc = side_acc + dot(patch, w, 1, 1)
    scale_row, shift_row = rows[2:3], rows[3:4]
    value, slope = act_parts(scale_row * side_acc + shift_row)
    act_out[MID:, :MID] = (side_mask[...] * value).astype(BF16)
    act_out[MID:, MID:] = jnp.zeros((16, OWN - MID), BF16)
    side_slope[...] = (scale_row * side_mask[...]) * slope
    mask = tile_mask(tissue[pl.ds(me[0], 1), :])
    for lo in range(0, MID, 32):
        part = slice(lo, lo + 32)
        scale = cols[part, 2:3]
        shift = cols[part, 3:4]
        for r in range(ROWS):
            seg = slice(r * WIDE, (r + 1) * WIDE)
            value, slope = act_parts(scale * acc[part, seg] + shift)
            act_out[part, seg] = (mask * value).astype(BF16)
            slope_out[part, seg] = (scale * mask) * slope


def expand_kernel(me, s0, s1, s2, s3, weight, feat, ups, scales, shifts, tissue, west, east, out, err_out, b0, b1, b2, b3, grad_out, acc, back):
    g = me[0]
    par = jnp.concatenate([scales[...], shifts[...], jnp.zeros((126, CH), F32)], 0).T
    cells = [jnp.zeros((16, MID), F32)] * 2
    group = lax.broadcasted_iota(jnp.int32, (16, MID), 0) // 4
    for k, s in enumerate((s0, s1, s2, s3)):
        q = (g + N_GRP - k) % N_GRP
        tail = s[MID:, :MID].astype(F32)
        for n in range(2):
            cells[n] = jnp.where(group == q, jnp.concatenate([tail[8 * n : 8 * n + 4]] * 4, 0), cells[n])
    scale_row, shift_row = scales[...], shifts[...]
    wide = dot(jnp.concatenate(cells, 0).astype(BF16), weight[...], 1, 1)
    errs = []
    for n, (strip, flag) in enumerate(zip((west, east), side_flags(me))):
        pre = strip[:16].astype(F32) + scale_row * wide[16 * n : 16 * n + 16] + shift_row
        _, slope = act_parts(pre)
        errs.append(scale_row * (slope * (strip[48:].astype(F32) * flag) * strip[32:48].astype(F32)))
    sides = dot(jnp.concatenate(errs, 0).astype(BF16), weight[...])
    blank = jnp.zeros((4, MID), F32)
    grad = None
    for k, (s, b_out) in enumerate(((s0, b0), (s1, b1), (s2, b2), (s3, b3))):
        q = (g + N_GRP - k) % N_GRP
        base = pl.multiple_of(q * OWN, OWN)
        acc[...] = dot(weight[...], s[:MID])
        mine = pick_rows(sides, q, 2)
        b_out[MID:, :MID] = jnp.concatenate([mine[:4], blank, mine[4:], blank], 0).astype(BF16)
        b_out[MID:, MID:] = jnp.zeros((16, OWN - MID), BF16)
        mask = tile_mask(tissue[pl.ds(q, 1), :])
        for lo in range(0, CH, 32):
            part = slice(lo, lo + 32)
            scale = par[part, 0:1]
            shift = par[part, 1:2]
            for r in range(ROWS):
                seg = pl.ds(pl.multiple_of(base + r * WIDE, WIDE), WIDE)
                here = slice(r * WIDE, (r + 1) * WIDE)
                pre = feat[part, seg].astype(F32) + scale * acc[part, here] + shift
                value, slope = act_parts(pre)
                err = slope * (mask * ups[part, seg].astype(F32))
                out[part, seg] = (mask * value).astype(BF16)
                err_out[part, seg] = err.astype(BF16)
                back[part, here] = (scale * err).astype(BF16)
        b_out[:MID] = dot(weight[...], back[...], 0, 0).astype(BF16)
        term = dot(back[...], s[:MID], 1, 1)
        grad = term if grad is None else grad + term
    put_matrix(grad_out, grad)


def put_matrix(out, matrix):
    for p in range(8):
        q, h = divmod(p, 2)
        out[p] = matrix[q * MAT_ROWS : (q + 1) * MAT_ROWS, h * WIDE : (h + 1) * WIDE].astype(BF16)


def pack_kernel(owner, out, packed):
    row_own = jnp.broadcast_to(owner[...], (WIDE, WIDE))
    sub = lax.broadcasted_iota(jnp.int32, (WIDE, WIDE), 0)
    lane = lanes((WIDE, WIDE))
    col_own = jnp.sum(jnp.where(sub == lane, row_own, 0), 1, keepdims=True)
    rank = jnp.sum(jnp.where((col_own == row_own) & (lane < sub), 1, 0), 1, keepdims=True)
    slot = jnp.broadcast_to(col_own * 4 + rank, (WIDE, WIDE))
    pick = lane % 64
    cell = 4 * (pick // 2) + 2 * (pick % 2)
    even = (sub == cell + lane // 64).astype(BF16)
    odd = (sub == cell + 1 - lane // 64).astype(BF16)
    target = []
    for x in range(N_GRP):
        mine = jnp.where(sub == x * TILE_COLS + pick // 2, slot, 0)
        spot = jnp.sum(mine, 0, keepdims=True) * 4 + pick[:1] % 2
        target.append(spot)
    upper = lanes((1, WIDE)) // 64
    low = lanes((CH, WIDE)) < 64
    for j in range(2):
        goal = jnp.concatenate([t + 2 * ((upper + j) % 2) for t in target], 1)
        column = lax.broadcasted_iota(jnp.int32, (4 * CH, OWN), 0)
        select = (column == goal).astype(F32).astype(BF16)
        for i in range(2):
            pieces = []
            for x in range(N_GRP):
                at = x * OWN + i * WIDE
                first = dot(out[:, at : at + WIDE], even)
                second = dot(out[:, at + 2 * WIDE : at + 3 * WIDE], odd)
                if j == 0:
                    pieces.append(jnp.where(low, first, second).astype(BF16))
                else:
                    pieces.append(jnp.where(low, second, first).astype(BF16))
            moved = dot(select, jnp.concatenate(pieces, 1), 1, 1).astype(BF16)
            ij = 2 * i + j
            for h in range(2):
                packed[:, h * 512 + ij * WIDE : h * 512 + (ij + 1) * WIDE] = moved[:, h * WIDE : (h + 1) * WIDE]


def unpack_kernel(packed, out):
    row = lax.broadcasted_iota(jnp.int32, (512, 512), 0)
    col = lanes((512, 512))
    order = (col == (row % 4) * WIDE + row // 4).astype(F32).astype(BF16)
    for h in range(2):
        part = slice(h * 512, (h + 1) * 512)
        out[part] = dot(order, packed[:, part], 1, 1).astype(BF16)


def back_second_kernel(b0, b1, b2, b3, slope, side_slope, grid_out, side_out, north_out, south_out):
    tails = [b[MID:, :MID].astype(F32) for b in (b0, b1, b2, b3)]
    side_out[...] = (side_slope[...] * ((tails[0] + tails[1]) + (tails[2] + tails[3]))).astype(BF16)
    for lo in range(0, MID, 32):
        part = slice(lo, lo + 32)
        total = (b0[part].astype(F32) + b1[part].astype(F32)) + (b2[part].astype(F32) + b3[part].astype(F32))
        grid_out[part] = (slope[part] * total).astype(BF16)
    put_edges(grid_out, side_out, north_out, south_out)


def back_first_kernel(me, grid, side, above, below, mine, other, slope, back_out, win, acc):
    shifted(me, grid, side, above, below, win)
    for t, (a, b) in enumerate(TAPS):
        w = tap_weight(me, mine, other, t)
        start = (1 - a) * WIDE
        part = dot(w, win[1 - b, :, start : start + OWN], 0, 0)
        acc[...] = part if t == 0 else acc[...] + part
    back_out[...] = (slope[...] * acc[...]).astype(BF16)


def spatial_kernel(me, grid, win, expand_part, keep, send):
    core = me[1] % 2
    for t, (a, b) in enumerate(TAPS):
        start = (a + 1) * WIDE
        term = dot(grid[...], win[b + 1, :, start : start + OWN], 1, 1)
        lo, hi = term[:, :WIDE], term[:, WIDE:]
        mine = jnp.where(core == 0, lo, hi).astype(BF16)
        other = jnp.where(core == 0, hi, lo).astype(BF16)
        for q in range(N_GRP):
            for at in range(0, 64, 16):
                block, within = divmod(t * 64 + at, SP_ROWS)
                rows = slice(q * SP_ROWS + within, q * SP_ROWS + within + 16)
                keep[block, rows] = mine[q * 64 + at : q * 64 + at + 16]
                send[block, rows] = other[q * 64 + at : q * 64 + at + 16]
    for block in range(4):
        keep[block, N_GRP * SP_ROWS :] = expand_part[2 * block + core]
        send[block, N_GRP * SP_ROWS :] = expand_part[2 * block + 1 - core]


def pair_sum_kernel(me, keep, got, y0, y1, y2, y3):
    row = me[1] // 2 % 4
    for k, out in enumerate((y0, y1, y2, y3)):
        q = (row + k) % 4
        out[...] = (keep[q].astype(F32) + got[q].astype(F32)).astype(BF16)


def row_sum_kernel(me, y0, y1, y2, y3, x0, x1, x2, x3, matrix):
    def total(rows):
        return (
            (y0[rows].astype(F32) + y1[rows].astype(F32)) + (y2[rows].astype(F32) + y3[rows].astype(F32))
        ).astype(BF16)

    for k, out in enumerate((x0, x1, x2, x3)):
        start = pl.multiple_of(((me[0] + k) % N_GRP) * SP_ROWS, 16)
        out[...] = total(pl.ds(start, SP_ROWS))
    matrix[...] = total(slice(N_GRP * SP_ROWS, N_GRP * SP_ROWS + MAT_ROWS))


def last_kernel(me, o0, o1, o2, o3, weight, feat, err, out, grad_out, send):
    g = me[0]
    grad = None
    for k, o in enumerate((o0, o1, o2, o3)):
        base = pl.multiple_of(((g + N_GRP - k) % N_GRP) * OWN, OWN)
        seg = pl.ds(base, OWN)
        out[:, seg] = (err[:, seg].astype(F32) + dot(weight[...], o[...], 0, 0)).astype(BF16)
        term = dot(o[...], feat[:, seg], 1, 1)
        grad = term if grad is None else grad + term
    put_matrix(grad_out, grad)
    core = me[1] % 2
    for q in range(4):
        send[q] = grad_out[2 * q + 1 - core]


def pair_matrix_kernel(me, part, got, y0, y1, y2, y3):
    core = me[1] % 2
    row = me[1] // 2 % 4
    for k, out in enumerate((y0, y1, y2, y3)):
        q = (row + k) % 4
        out[...] = (part[2 * q + core].astype(F32) + got[q].astype(F32)).astype(BF16)


def plane_sum_kernel(x0, x1, x2, x3, expand_part, y0, y1, y2, y3, out):
    spatial = (x0[...].astype(F32) + x1[...].astype(F32)) + (x2[...].astype(F32) + x3[...].astype(F32))
    total = (y0[...].astype(F32) + y1[...].astype(F32)) + (y2[...].astype(F32) + y3[...].astype(F32))
    spatial = spatial.astype(BF16)
    total = total.astype(BF16)
    out[:SP_ROWS] = spatial
    out[SP_ROWS : SP_ROWS + MAT_ROWS] = expand_part[...]
    out[SP_ROWS + MAT_ROWS :] = total


def two_sum_kernel(one, two, out):
    out[...] = (one[...].astype(F32) + two[...].astype(F32)).astype(BF16)


def all_sum_kernel(*refs):
    parts, out = refs[:-1], refs[-1]
    total = parts[0][...].astype(F32)
    for part in parts[1:]:
        total = total + part[...].astype(F32)
    total = total.astype(BF16)
    for p in range(8):
        out[p] = total


def finish_kernel(parts, reduce_out, spatial_out, expand_out):
    for p in range(8):
        q, h = divmod(p, 2)
        seg = slice(h * WIDE, (h + 1) * WIDE)
        spatial_out[q * SP_ROWS : (q + 1) * SP_ROWS, seg] = parts[p, :SP_ROWS].astype(F32) * GRAD_SCALE
        rows = slice(q * MAT_ROWS, (q + 1) * MAT_ROWS)
        expand_out[rows, seg] = parts[p, SP_ROWS : SP_ROWS + MAT_ROWS].astype(F32) * GRAD_SCALE
        reduce_out[rows, seg] = parts[p, SP_ROWS + MAT_ROWS :].astype(F32) * GRAD_SCALE


def along_grp(block, step):
    return lax.ppermute(block, "grp", [(i, (i + step) % N_GRP) for i in range(N_GRP)])


def pair_swap(block):
    return lax.ppermute(block, "slide", [(d, d ^ 1) for d in range(N_SLIDE)])


def along_row(block, step):
    moves = [(d, d // 8 * 8 + (d + 2 * step) % 8) for d in range(N_SLIDE)]
    return lax.ppermute(block, "slide", moves)


def column_swap(block):
    return lax.ppermute(block, "slide", [(d, d ^ 8) for d in range(N_SLIDE)])


def along_column(block, step):
    return lax.ppermute(block, "slide", [(d, (d + 8 * step) % N_SLIDE) for d in range(N_SLIDE)])


def beside(block, step):
    moves = [(d, d // GRID_C * GRID_C + (d + step) % GRID_C) for d in range(N_SLIDE)]
    return lax.ppermute(block, "slide", moves)


def line_moves(step):
    moves = []
    for d in range(N_SLIDE):
        for g in range(N_GRP):
            line = (d // GRID_C * N_GRP + g + step) % (GRID_R * N_GRP)
            there = line // N_GRP * GRID_C + d % GRID_C
            moves.append((d * N_GRP + g, there * N_GRP + line % N_GRP))
    return moves


def halo(north, south):
    above = lax.ppermute(south, ("slide", "grp"), line_moves(1))
    below = lax.ppermute(north, ("slide", "grp"), line_moves(-1))
    return above, below


PLANE = [[z * 8 + k for k in range(8)] for z in range(8)]


def exchange(pieces, groups):
    return lax.all_to_all(
        pieces, "slide", split_axis=0, concat_axis=0, axis_index_groups=groups, tiled=False
    )


def shards(
    features,
    tissue,
    group_owner,
    reduce_weight,
    spatial_weight,
    expand_weight,
    reduce_scale,
    reduce_shift,
    spatial_scale,
    spatial_shift,
    expand_scale,
    expand_shift,
    upstream,
):
    me = jnp.stack([lax.axis_index("grp"), lax.axis_index("slide")]).astype(jnp.int32)
    own = (MID, OWN)
    long = (MID + PARAM_ROWS, OWN)
    side = (16, MID)
    edge = [((MID + 16, WIDE), BF16)] * 2
    half = spatial_weight.shape[1] // 2
    quarter = lax.dynamic_slice_in_dim(spatial_weight, lax.axis_index("slide") % 2 * half, half, 1)
    quarters = [quarter] + [along_grp(quarter, k) for k in (1, 2, 3)]
    strips = call(strip_kernel, [((64, CH), BF16)] * 2, features, upstream, tissue, flops=4 * WIDE * CH * CELLS)
    east, west = beside(strips[0], -1), beside(strips[1], 1)
    mine, = call(weights_kernel, [((N_GRP,) + quarter.shape, BF16)], me, *quarters, smem=(0,), after=(east, west))
    other = pair_swap(mine)
    scales = jnp.stack([reduce_scale, reduce_shift, spatial_scale, spatial_shift])
    with jax.named_scope("reduce"):
        p = call(
            reduce_kernel,
            [(long, BF16)] * 4,
            me, features, reduce_weight, scales, west, east,
            smem=(0,), flops=2 * MID * CH * CELLS, after=(mine,),
        )
        p = [p[0]] + [along_grp(p[k], k) for k in (1, 2, 3)]
    with jax.named_scope("first"):
        first, slope_one, cols, rows, side_one, side_mask, *edges = call(
            first_kernel,
            [(own, BF16), (own, F32), ((MID, WIDE), F32), ((8, MID), F32), (side, BF16), (side, F32)] + edge,
            me, *p, tissue, west, east,
            smem=(0,), flops=40 * MID * OWN, after=(other,),
        )
        edges = halo(*edges)
    with jax.named_scope("second"):
        second, slope_two, side_slope, win = call(
            second_kernel,
            [(long, BF16), (own, F32), (side, F32), ((3, MID, OWN + 2 * WIDE), BF16)],
            me, first, side_one, *edges, mine, other, cols, rows, side_mask, tissue,
            smem=(0,), flops=18 * MID * MID * OWN, scratch=[pltpu.VMEM(own, F32)],
        )
        s = [second] + [along_grp(second, k) for k in (1, 2, 3)]
    with jax.named_scope("expand"):
        output, err, b0, b1, b2, b3, expand_part = call(
            expand_kernel,
            [((CH, CELLS), BF16), ((CH, CELLS), BF16)] + [(long, BF16)] * 4 + [((8, MAT_ROWS, WIDE), BF16)],
            me, *s, expand_weight, features, upstream, expand_scale.reshape(1, -1), expand_shift.reshape(1, -1), tissue, west, east,
            smem=(0,), flops=6 * CH * MID * CELLS,
            scratch=[pltpu.VMEM(own, F32), pltpu.VMEM(own, BF16)],
        )
        b = [b0] + [along_grp(v, -k) for k, v in ((1, b1), (2, b2), (3, b3))]
    with jax.named_scope("merge"):
        packed, = call(
            pack_kernel, [((4 * CH, 4 * CH), BF16)], group_owner.reshape(1, -1), output,
            flops=8 * CH * 4 * CH * OWN,
        )
    with jax.named_scope("back_second"):
        back_two, side_two, *edges = call(
            back_second_kernel,
            [(own, BF16), (side, BF16)] + edge,
            *b, slope_two, side_slope, flops=10 * MID * OWN, after=(packed,),
        )
        edges = halo(*edges)
    with jax.named_scope("spatial"):
        half = (4, N_GRP * SP_ROWS + MAT_ROWS, WIDE)
        keep, send = call(
            spatial_kernel, [(half, BF16)] * 2, me, back_two, win, expand_part,
            smem=(0,), flops=18 * MID * MID * OWN,
        )
        y = call(pair_sum_kernel, [(half[1:], BF16)] * 4, me, keep, pair_swap(send), smem=(0,))
    with jax.named_scope("back_first"):
        back_one, = call(
            back_first_kernel,
            [(own, BF16)],
            me, back_two, side_two, *edges, mine, other, slope_one,
            smem=(0,), flops=18 * MID * MID * OWN,
            scratch=[pltpu.VMEM((3, MID, OWN + 2 * WIDE), BF16), pltpu.VMEM(own, F32)],
        )
        o = [back_one] + [along_grp(back_one, k) for k in (1, 2, 3)]
    with jax.named_scope("merge"):
        packed = gate(packed, back_one, y[0])
        arrived = lax.all_to_all(
            packed.reshape(N_SLIDE, 16, 4 * CH), "slide", split_axis=0, concat_axis=0, tiled=False
        ).reshape(4 * CH, 4 * CH)
    with jax.named_scope("spatial"):
        y = [y[0]] + [along_row(y[k], k) for k in (1, 2, 3)]
        *x, expand_part = call(
            row_sum_kernel, [((SP_ROWS, WIDE), BF16)] * 4 + [((MAT_ROWS, WIDE), BF16)],
            me, *y, smem=(0,),
        )
    with jax.named_scope("early"):
        x = [x[0]] + [along_grp(x[k], k) for k in (1, 2, 3)]
    with jax.named_scope("last"):
        feature_grad, reduce_part, send = call(
            last_kernel,
            [((CH, CELLS), BF16), ((8, MAT_ROWS, WIDE), BF16), ((4, MAT_ROWS, WIDE), BF16)],
            me, *o, reduce_weight, features, err,
            smem=(0,), flops=4 * CH * MID * CELLS,
        )
    with jax.named_scope("merge"):
        merged, = call(
            unpack_kernel, [((4 * CH, 4 * CH), BF16)], arrived,
            flops=4 * 512 * 512 * 4 * CH,
        )
    with jax.named_scope("grads"):
        y = call(
            pair_matrix_kernel, [((MAT_ROWS, WIDE), BF16)] * 4, me, reduce_part, pair_swap(send), smem=(0,)
        )
        y = [y[0]] + [along_row(y[k], k) for k in (1, 2, 3)]
        spread = ((8, SP_ROWS + 2 * MAT_ROWS, WIDE), BF16)
        plane, = call(plane_sum_kernel, [(spread[0][1:], BF16)], *x, expand_part, *y)
        plane, = call(two_sum_kernel, [(spread[0][1:], BF16)], plane, column_swap(plane))
        total, = call(all_sum_kernel, [spread], plane, *[along_column(plane, k) for k in (2, 4, 6)], after=(arrived,))
        reduce_grad, spatial_grad, expand_grad = call(
            finish_kernel,
            [((MID, CH), F32), ((9 * 64, MID), F32), ((CH, MID), F32)],
            exchange(total, PLANE),
        )
    return merged, feature_grad, reduce_grad, spatial_grad.reshape(9, 64, MID), expand_grad


def solution(mesh):
    return jax.shard_map(
        shards,
        mesh=mesh,
        in_specs=(
            P("grp", "slide"),
            P("slide", None),
            P("slide", None),
            P(None, "grp"),
            P(None, "grp", None),
            P("grp", None),
            P("grp"),
            P("grp"),
            P("grp"),
            P("grp"),
            P("grp"),
            P("grp"),
            P("grp", "slide"),
        ),
        out_specs=(
            P("grp", "slide"),
            P("grp", "slide"),
            P(None, "grp"),
            P(None, "grp", None),
            P("grp", None),
        ),
        check_vma=False,
    )
```

```python
import functools
import math

import jax
import jax.numpy as jnp
from jax import lax
from jax.experimental import pallas as pl
from jax.experimental.pallas import tpu as pltpu
from jax.sharding import PartitionSpec as P

F32 = jnp.float32
BF16 = jnp.bfloat16
KAPPA = math.sqrt(2.0 / math.pi)
CUBIC = 0.044715
VMEM_BYTES = 48 * 1024 * 1024

GRID_R = 8
GRID_C = 8
N_SLIDE = 64
N_GRP = 4
TILE_COLS = 32
WIDE = 128
ROWS = 4
OWN = ROWS * WIDE
CELLS = N_GRP * OWN
CH = 256
MID = 256
PARAM_ROWS = 16
TAPS = tuple((a, b) for a in (-1, 0, 1) for b in (-1, 0, 1))
GRAD_SCALE = 1.0 / math.sqrt(N_SLIDE * CELLS)
SP_ROWS = 144
MAT_ROWS = 64


def call(body, outs, *args, flops=0, scratch=(), smem=(), after=()):
    spec = pl.BlockSpec()
    scalar = pl.BlockSpec(memory_space=pltpu.SMEM)
    moved = sum(math.prod(s) * jnp.dtype(d).itemsize for s, d in outs)
    moved += sum(math.prod(a.shape) * a.dtype.itemsize for a in args)
    held = len(args)

    def ordered(*refs):
        body(*refs[:held], *refs[held + len(after) :])

    return pl.pallas_call(
        ordered,
        out_shape=[jax.ShapeDtypeStruct(s, d) for s, d in outs],
        in_specs=[scalar if i in smem else spec for i in range(held)]
        + [pl.BlockSpec(memory_space=pl.ANY)] * len(after),
        out_specs=[spec] * len(outs),
        scratch_shapes=list(scratch),
        compiler_params=pltpu.CompilerParams(vmem_limit_bytes=VMEM_BYTES),
        cost_estimate=pl.CostEstimate(flops=flops, bytes_accessed=moved, transcendentals=0),
    )(*args, *after)


def gate(array, *after):
    place = pl.BlockSpec(memory_space=pl.ANY)
    return pl.pallas_call(
        lambda *refs: None,
        out_shape=jax.ShapeDtypeStruct(array.shape, array.dtype),
        in_specs=[place] * (1 + len(after)),
        out_specs=place,
        input_output_aliases={0: 0},
    )(array, *after)


def dot(lhs, rhs, left=1, right=0):
    return lax.dot_general(lhs, rhs, (((left,), (right,)), ((), ())), preferred_element_type=F32)


def act_parts(v):
    sq = v * v
    t = jnp.tanh(v * (KAPPA + (KAPPA * CUBIC) * sq))
    half = 0.5 + 0.5 * t
    value = v * half
    slope = half + (value * (1.0 - t)) * (KAPPA + (3.0 * KAPPA * CUBIC) * sq)
    return value, slope


def tile_mask(tissue_row):
    spread = (
        lax.broadcasted_iota(jnp.int32, (TILE_COLS, WIDE), 1) // 4
        == lax.broadcasted_iota(jnp.int32, (TILE_COLS, WIDE), 0)
    ).astype(F32)
    row = tissue_row.astype(F32)
    if row.shape[0] == 1:
        row = jnp.broadcast_to(row, (8, TILE_COLS))
    return dot(row, spread)[:1]


def lanes(shape):
    return lax.broadcasted_iota(jnp.int32, shape, len(shape) - 1)


def side_flags(me):
    col = me[1] % GRID_C
    return (col > 0).astype(F32), (col < GRID_C - 1).astype(F32)


def strip_kernel(feat, ups, tissue, left_out, right_out):
    place = lax.broadcasted_iota(jnp.int32, (WIDE, CELLS), 0)
    cell = lanes((WIDE, CELLS))
    kind, row = place % 64 // 16, place % 16
    col = jnp.where(place < 64, kind, WIDE - 1 - kind)
    edge = jnp.where(place < 64, 0, WIDE - 1)
    here = cell // WIDE == row
    pick = (here & (cell % WIDE == col) & (kind < 2)).astype(F32).astype(BF16)
    pick_ups = (here & (cell % WIDE == edge) & (kind == 2)).astype(F32).astype(BF16)
    strips = dot(pick, feat[...], 1, 1) + dot(pick_ups, ups[...], 1, 1)
    tiles = tissue[...].astype(F32)
    for out, lo, at in ((left_out, 0, 0), (right_out, 64, TILE_COLS - 1)):
        out[:48] = strips[lo : lo + 48].astype(BF16)
        flags = [jnp.broadcast_to(tiles[q : q + 1, at : at + 1], (4, CH)) for q in range(N_GRP)]
        out[48:] = jnp.concatenate(flags, 0).astype(BF16)


def reduce_kernel(me, feat, weight, scales, west, east, *outs):
    g = me[0]
    par = jnp.concatenate([scales[...]] * N_GRP, 1)
    par = jnp.where(lanes((4, MID)) // (MID // N_GRP) == g, par, 0.0)
    hi = par.astype(BF16)
    rest = par - hi.astype(F32)
    mid = rest.astype(BF16)
    low = (rest - mid.astype(F32)).astype(BF16)
    tail = jnp.concatenate(
        [hi.astype(F32), mid.astype(F32), low.astype(F32), jnp.zeros((4, MID), F32)], 0
    ).astype(BF16)
    sides = dot(jnp.concatenate([west[:32], east[:32]], 0), weight[...], 1, 1)
    for k in range(N_GRP):
        q = (g + k) % N_GRP
        start = pl.multiple_of(q * OWN, OWN)
        block = dot(weight[...], feat[:, pl.ds(start, OWN)])
        outs[k][:MID] = block.astype(BF16)
        outs[k][MID:, :MID] = tail
        mine = pick_rows(sides, q, 4)
        outs[k][MID:, MID:] = mine.astype(BF16)


def pick_rows(cells, q, groups):
    picked = []
    for n in range(groups):
        rows = jnp.zeros((4, cells.shape[1]), F32)
        for j in range(N_GRP):
            rows = jnp.where(q == j, cells[n * 16 + 4 * j : n * 16 + 4 * j + 4], rows)
        picked.append(rows)
    return jnp.concatenate(picked, 0)


def weights_kernel(me, w0, w1, w2, w3, out):
    for k, w in enumerate((w0, w1, w2, w3)):
        out[(me[0] + N_GRP - k) % N_GRP] = w[...]


def tap_weight(me, mine, other, t):
    core = me[1] % 2
    rows = []
    for q in range(N_GRP):
        here, there = mine[q, t], other[q, t]
        rows += [jnp.where(core == 0, here, there), jnp.where(core == 0, there, here)]
    return jnp.concatenate(rows, 0)


def first_kernel(
    me, p0, p1, p2, p3, tissue, west, east,
    act_out, slope_out, cols_out, rows_out, side_out, side_mask, north_out, south_out,
):
    g = me[0]
    tails = [p[MID:].astype(F32) for p in (p0, p1, p2, p3)]
    rows = (tails[0] + tails[1]) + (tails[2] + tails[3])
    par = (rows[0:4, :MID] + rows[4:8, :MID]) + rows[8:12, :MID]
    rows_out[...] = jnp.concatenate([par, jnp.zeros((4, MID), F32)], 0)
    cols = jnp.concatenate([par, jnp.zeros((124, MID), F32)], 0).T
    cols_out[...] = cols
    lhs, rhs = side_flags(me)
    west_mask = pick_rows(west[48:].astype(F32), g, 1) * lhs
    east_mask = pick_rows(east[48:].astype(F32), g, 1) * rhs
    flags = jnp.concatenate([west_mask, west_mask, east_mask, east_mask], 0)
    side_mask[...] = flags
    side, _ = act_parts(par[0:1] * rows[:, MID:] + par[1:2])
    side_out[...] = (flags * side).astype(BF16)
    mask = tile_mask(tissue[pl.ds(g, 1), :])
    for lo in range(0, MID, 32):
        part = slice(lo, lo + 32)
        scale = cols[part, 0:1]
        shift = cols[part, 1:2]
        for r in range(ROWS):
            seg = slice(r * WIDE, (r + 1) * WIDE)
            total = (p0[part, seg].astype(F32) + p1[part, seg].astype(F32)) + (
                p2[part, seg].astype(F32) + p3[part, seg].astype(F32)
            )
            value, slope = act_parts(scale * total + shift)
            act_out[part, seg] = (mask * value).astype(BF16)
            slope_out[part, seg] = (scale * mask) * slope
    put_edges(act_out, side_out, north_out, south_out)


def put_edges(grid, side, north_out, south_out):
    cells = side[...].astype(F32)
    for out, r in ((north_out, 0), (south_out, ROWS - 1)):
        out[:MID] = grid[:, r * WIDE : (r + 1) * WIDE]
        lines = []
        for n in range(4):
            cell = cells[4 * n + r : 4 * n + r + 1]
            lines += [cell[:, :WIDE], cell[:, WIDE:]]
        out[MID:] = jnp.concatenate(lines + [jnp.zeros((8, WIDE), F32)], 0).astype(BF16)


def side_rows(me, side, above, below):
    g, s = me[0], me[1]
    north = ((g > 0) | (s >= GRID_C)).astype(F32)
    south = ((g < N_GRP - 1) | (s < N_SLIDE - GRID_C)).astype(F32)
    cells = side[...].astype(F32)
    up = above[MID:].astype(F32) * north
    down = below[MID:].astype(F32) * south
    kinds = []
    for n in range(4):
        first = jnp.concatenate([up[2 * n : 2 * n + 1], up[2 * n + 1 : 2 * n + 2]], 1)
        last = jnp.concatenate([down[2 * n : 2 * n + 1], down[2 * n + 1 : 2 * n + 2]], 1)
        kinds.append(jnp.concatenate([first, cells[4 * n : 4 * n + 4], last], 0))
    return north, south, kinds


def shifted(me, grid, side, above, below, out):
    north, south, kinds = side_rows(me, side, above, below)
    columns = jnp.concatenate(
        [kinds[0], kinds[2], jnp.zeros((WIDE - 2 * (ROWS + 2), MID), F32)], 0
    ).T
    lane = lanes((MID, WIDE))
    for r in range(ROWS + 2):
        seg = slice(r * WIDE, (r + 1) * WIDE)
        if r == 0:
            row = above[:MID].astype(F32) * north
        elif r == ROWS + 1:
            row = below[:MID].astype(F32) * south
        else:
            row = grid[:, (r - 1) * WIDE : r * WIDE].astype(F32)
        lcol = columns[:, r : r + 1]
        rcol = columns[:, ROWS + 2 + r : ROWS + 3 + r]
        out[1, :, seg] = row.astype(BF16)
        out[0, :, seg] = jnp.where(lane == 0, lcol, pltpu.roll(row, 1, 1)).astype(BF16)
        out[2, :, seg] = jnp.where(lane == WIDE - 1, rcol, pltpu.roll(row, WIDE - 1, 1)).astype(BF16)
    return kinds


def second_kernel(
    me, grid, side, above, below, mine, other, cols, rows, side_mask, tissue,
    act_out, slope_out, side_slope, win_out, acc,
):
    near_west, next_west, near_east, next_east = shifted(me, grid, side, above, below, win_out)
    ends = (
        lanes((16, WIDE)) == (WIDE - 1) * (lax.broadcasted_iota(jnp.int32, (16, WIDE), 0) // 8)
    ).astype(F32).astype(BF16)
    firsts, lasts = [], []
    for r in range(ROWS + 2):
        both = dot(ends, win_out[1, :, r * WIDE : (r + 1) * WIDE], 1, 1)
        firsts.append(both[0:1])
        lasts.append(both[8:9])
    first_col = jnp.concatenate(firsts, 0)
    last_col = jnp.concatenate(lasts, 0)
    blank = jnp.zeros((4, MID), F32)
    side_acc = jnp.zeros((16, MID), F32)
    for t, (a, b) in enumerate(TAPS):
        w = tap_weight(me, mine, other, t)
        start = (a + 1) * WIDE
        part = dot(w, win_out[b + 1, :, start : start + OWN])
        acc[...] = part if t == 0 else acc[...] + part
        lhs = (next_west, near_west, first_col)[b + 1][a + 1 : a + 5]
        rhs = (last_col, near_east, next_east)[b + 1][a + 1 : a + 5]
        patch = jnp.concatenate([lhs, blank, rhs, blank], 0).astype(BF16)
        side_acc = side_acc + dot(patch, w, 1, 1)
    scale_row, shift_row = rows[2:3], rows[3:4]
    value, slope = act_parts(scale_row * side_acc + shift_row)
    act_out[MID:, :MID] = (side_mask[...] * value).astype(BF16)
    act_out[MID:, MID:] = jnp.zeros((16, OWN - MID), BF16)
    side_slope[...] = (scale_row * side_mask[...]) * slope
    mask = tile_mask(tissue[pl.ds(me[0], 1), :])
    for lo in range(0, MID, 32):
        part = slice(lo, lo + 32)
        scale = cols[part, 2:3]
        shift = cols[part, 3:4]
        for r in range(ROWS):
            seg = slice(r * WIDE, (r + 1) * WIDE)
            value, slope = act_parts(scale * acc[part, seg] + shift)
            act_out[part, seg] = (mask * value).astype(BF16)
            slope_out[part, seg] = (scale * mask) * slope


def expand_kernel(me, s0, s1, s2, s3, weight, feat, ups, scales, shifts, tissue, west, east, out, err_out, b0, b1, b2, b3, grad_out, acc, back):
    g = me[0]
    par = jnp.concatenate([scales[...], shifts[...], jnp.zeros((126, CH), F32)], 0).T
    cells = [jnp.zeros((16, MID), F32)] * 2
    group = lax.broadcasted_iota(jnp.int32, (16, MID), 0) // 4
    for k, s in enumerate((s0, s1, s2, s3)):
        q = (g + N_GRP - k) % N_GRP
        tail = s[MID:, :MID].astype(F32)
        for n in range(2):
            cells[n] = jnp.where(group == q, jnp.concatenate([tail[8 * n : 8 * n + 4]] * 4, 0), cells[n])
    scale_row, shift_row = scales[...], shifts[...]
    wide = dot(jnp.concatenate(cells, 0).astype(BF16), weight[...], 1, 1)
    errs = []
    for n, (strip, flag) in enumerate(zip((west, east), side_flags(me))):
        pre = strip[:16].astype(F32) + scale_row * wide[16 * n : 16 * n + 16] + shift_row
        _, slope = act_parts(pre)
        errs.append(scale_row * (slope * (strip[48:].astype(F32) * flag) * strip[32:48].astype(F32)))
    sides = dot(jnp.concatenate(errs, 0).astype(BF16), weight[...])
    blank = jnp.zeros((4, MID), F32)
    grad = None
    for k, (s, b_out) in enumerate(((s0, b0), (s1, b1), (s2, b2), (s3, b3))):
        q = (g + N_GRP - k) % N_GRP
        base = pl.multiple_of(q * OWN, OWN)
        acc[...] = dot(weight[...], s[:MID])
        mine = pick_rows(sides, q, 2)
        b_out[MID:, :MID] = jnp.concatenate([mine[:4], blank, mine[4:], blank], 0).astype(BF16)
        b_out[MID:, MID:] = jnp.zeros((16, OWN - MID), BF16)
        mask = tile_mask(tissue[pl.ds(q, 1), :])
        for lo in range(0, CH, 32):
            part = slice(lo, lo + 32)
            scale = par[part, 0:1]
            shift = par[part, 1:2]
            for r in range(ROWS):
                seg = pl.ds(pl.multiple_of(base + r * WIDE, WIDE), WIDE)
                here = slice(r * WIDE, (r + 1) * WIDE)
                pre = feat[part, seg].astype(F32) + scale * acc[part, here] + shift
                value, slope = act_parts(pre)
                err = slope * (mask * ups[part, seg].astype(F32))
                out[part, seg] = (mask * value).astype(BF16)
                err_out[part, seg] = err.astype(BF16)
                back[part, here] = (scale * err).astype(BF16)
        b_out[:MID] = dot(weight[...], back[...], 0, 0).astype(BF16)
        term = dot(back[...], s[:MID], 1, 1)
        grad = term if grad is None else grad + term
    put_matrix(grad_out, grad)


def put_matrix(out, matrix):
    for p in range(8):
        q, h = divmod(p, 2)
        out[p] = matrix[q * MAT_ROWS : (q + 1) * MAT_ROWS, h * WIDE : (h + 1) * WIDE].astype(BF16)


def pack_kernel(owner, out, packed):
    row_own = jnp.broadcast_to(owner[...], (WIDE, WIDE))
    sub = lax.broadcasted_iota(jnp.int32, (WIDE, WIDE), 0)
    lane = lanes((WIDE, WIDE))
    col_own = jnp.sum(jnp.where(sub == lane, row_own, 0), 1, keepdims=True)
    rank = jnp.sum(jnp.where((col_own == row_own) & (lane < sub), 1, 0), 1, keepdims=True)
    slot = jnp.broadcast_to(col_own * 4 + rank, (WIDE, WIDE))
    pick = lane % 64
    cell = 4 * (pick // 2) + 2 * (pick % 2)
    even = (sub == cell + lane // 64).astype(BF16)
    odd = (sub == cell + 1 - lane // 64).astype(BF16)
    target = []
    for x in range(N_GRP):
        mine = jnp.where(sub == x * TILE_COLS + pick // 2, slot, 0)
        spot = jnp.sum(mine, 0, keepdims=True) * 4 + pick[:1] % 2
        target.append(spot)
    upper = lanes((1, WIDE)) // 64
    low = lanes((CH, WIDE)) < 64
    for j in range(2):
        goal = jnp.concatenate([t + 2 * ((upper + j) % 2) for t in target], 1)
        column = lax.broadcasted_iota(jnp.int32, (4 * CH, OWN), 0)
        select = (column == goal).astype(F32).astype(BF16)
        for i in range(2):
            pieces = []
            for x in range(N_GRP):
                at = x * OWN + i * WIDE
                first = dot(out[:, at : at + WIDE], even)
                second = dot(out[:, at + 2 * WIDE : at + 3 * WIDE], odd)
                if j == 0:
                    pieces.append(jnp.where(low, first, second).astype(BF16))
                else:
                    pieces.append(jnp.where(low, second, first).astype(BF16))
            moved = dot(select, jnp.concatenate(pieces, 1), 1, 1).astype(BF16)
            ij = 2 * i + j
            for h in range(2):
                packed[:, h * 512 + ij * WIDE : h * 512 + (ij + 1) * WIDE] = moved[:, h * WIDE : (h + 1) * WIDE]


def unpack_kernel(packed, out):
    row = lax.broadcasted_iota(jnp.int32, (512, 512), 0)
    col = lanes((512, 512))
    order = (col == (row % 4) * WIDE + row // 4).astype(F32).astype(BF16)
    for h in range(2):
        part = slice(h * 512, (h + 1) * 512)
        out[part] = dot(order, packed[:, part], 1, 1).astype(BF16)


def back_second_kernel(b0, b1, b2, b3, slope, side_slope, grid_out, side_out, north_out, south_out):
    tails = [b[MID:, :MID].astype(F32) for b in (b0, b1, b2, b3)]
    side_out[...] = (side_slope[...] * ((tails[0] + tails[1]) + (tails[2] + tails[3]))).astype(BF16)
    for lo in range(0, MID, 32):
        part = slice(lo, lo + 32)
        total = (b0[part].astype(F32) + b1[part].astype(F32)) + (b2[part].astype(F32) + b3[part].astype(F32))
        grid_out[part] = (slope[part] * total).astype(BF16)
    put_edges(grid_out, side_out, north_out, south_out)


def back_first_kernel(me, grid, side, above, below, mine, other, slope, back_out, win, acc):
    shifted(me, grid, side, above, below, win)
    for t, (a, b) in enumerate(TAPS):
        w = tap_weight(me, mine, other, t)
        start = (1 - a) * WIDE
        part = dot(w, win[1 - b, :, start : start + OWN], 0, 0)
        acc[...] = part if t == 0 else acc[...] + part
    back_out[...] = (slope[...] * acc[...]).astype(BF16)


def spatial_kernel(me, grid, win, expand_part, keep, send):
    core = me[1] % 2
    for t, (a, b) in enumerate(TAPS):
        start = (a + 1) * WIDE
        term = dot(grid[...], win[b + 1, :, start : start + OWN], 1, 1)
        lo, hi = term[:, :WIDE], term[:, WIDE:]
        mine = jnp.where(core == 0, lo, hi).astype(BF16)
        other = jnp.where(core == 0, hi, lo).astype(BF16)
        for q in range(N_GRP):
            for at in range(0, 64, 16):
                block, within = divmod(t * 64 + at, SP_ROWS)
                rows = slice(q * SP_ROWS + within, q * SP_ROWS + within + 16)
                keep[block, rows] = mine[q * 64 + at : q * 64 + at + 16]
                send[block, rows] = other[q * 64 + at : q * 64 + at + 16]
    for block in range(4):
        keep[block, N_GRP * SP_ROWS :] = expand_part[2 * block + core]
        send[block, N_GRP * SP_ROWS :] = expand_part[2 * block + 1 - core]


def pair_sum_kernel(me, keep, got, y0, y1, y2, y3):
    row = me[1] // 2 % 4
    for k, out in enumerate((y0, y1, y2, y3)):
        q = (row + k) % 4
        out[...] = (keep[q].astype(F32) + got[q].astype(F32)).astype(BF16)


def row_sum_kernel(me, y0, y1, y2, y3, x0, x1, x2, x3, matrix):
    def total(rows):
        return (
            (y0[rows].astype(F32) + y1[rows].astype(F32)) + (y2[rows].astype(F32) + y3[rows].astype(F32))
        ).astype(BF16)

    for k, out in enumerate((x0, x1, x2, x3)):
        start = pl.multiple_of(((me[0] + k) % N_GRP) * SP_ROWS, 16)
        out[...] = total(pl.ds(start, SP_ROWS))
    matrix[...] = total(slice(N_GRP * SP_ROWS, N_GRP * SP_ROWS + MAT_ROWS))


def last_kernel(me, o0, o1, o2, o3, weight, feat, err, out, grad_out, send):
    g = me[0]
    grad = None
    for k, o in enumerate((o0, o1, o2, o3)):
        base = pl.multiple_of(((g + N_GRP - k) % N_GRP) * OWN, OWN)
        seg = pl.ds(base, OWN)
        out[:, seg] = (err[:, seg].astype(F32) + dot(weight[...], o[...], 0, 0)).astype(BF16)
        term = dot(o[...], feat[:, seg], 1, 1)
        grad = term if grad is None else grad + term
    put_matrix(grad_out, grad)
    core = me[1] % 2
    for q in range(4):
        send[q] = grad_out[2 * q + 1 - core]


def pair_matrix_kernel(me, part, got, y0, y1, y2, y3):
    core = me[1] % 2
    row = me[1] // 2 % 4
    for k, out in enumerate((y0, y1, y2, y3)):
        q = (row + k) % 4
        out[...] = (part[2 * q + core].astype(F32) + got[q].astype(F32)).astype(BF16)


def plane_sum_kernel(x0, x1, x2, x3, expand_part, y0, y1, y2, y3, out):
    spatial = (x0[...].astype(F32) + x1[...].astype(F32)) + (x2[...].astype(F32) + x3[...].astype(F32))
    total = (y0[...].astype(F32) + y1[...].astype(F32)) + (y2[...].astype(F32) + y3[...].astype(F32))
    spatial = spatial.astype(BF16)
    total = total.astype(BF16)
    out[:SP_ROWS] = spatial
    out[SP_ROWS : SP_ROWS + MAT_ROWS] = expand_part[...]
    out[SP_ROWS + MAT_ROWS :] = total


def two_sum_kernel(one, two, out):
    out[...] = (one[...].astype(F32) + two[...].astype(F32)).astype(BF16)


def all_sum_kernel(*refs):
    parts, out = refs[:-1], refs[-1]
    total = parts[0][...].astype(F32)
    for part in parts[1:]:
        total = total + part[...].astype(F32)
    total = total.astype(BF16)
    for p in range(8):
        out[p] = total


def finish_kernel(parts, reduce_out, spatial_out, expand_out):
    for p in range(8):
        q, h = divmod(p, 2)
        seg = slice(h * WIDE, (h + 1) * WIDE)
        spatial_out[q * SP_ROWS : (q + 1) * SP_ROWS, seg] = parts[p, :SP_ROWS].astype(F32) * GRAD_SCALE
        rows = slice(q * MAT_ROWS, (q + 1) * MAT_ROWS)
        expand_out[rows, seg] = parts[p, SP_ROWS : SP_ROWS + MAT_ROWS].astype(F32) * GRAD_SCALE
        reduce_out[rows, seg] = parts[p, SP_ROWS + MAT_ROWS :].astype(F32) * GRAD_SCALE


def along_grp(block, step):
    return lax.ppermute(block, "grp", [(i, (i + step) % N_GRP) for i in range(N_GRP)])


def pair_swap(block):
    return lax.ppermute(block, "slide", [(d, d ^ 1) for d in range(N_SLIDE)])


def along_row(block, step):
    moves = [(d, d // 8 * 8 + (d + 2 * step) % 8) for d in range(N_SLIDE)]
    return lax.ppermute(block, "slide", moves)


def column_swap(block):
    return lax.ppermute(block, "slide", [(d, d ^ 8) for d in range(N_SLIDE)])


def along_column(block, step):
    return lax.ppermute(block, "slide", [(d, (d + 8 * step) % N_SLIDE) for d in range(N_SLIDE)])


def beside(block, step):
    moves = [(d, d // GRID_C * GRID_C + (d + step) % GRID_C) for d in range(N_SLIDE)]
    return lax.ppermute(block, "slide", moves)


def line_moves(step):
    moves = []
    for d in range(N_SLIDE):
        for g in range(N_GRP):
            line = (d // GRID_C * N_GRP + g + step) % (GRID_R * N_GRP)
            there = line // N_GRP * GRID_C + d % GRID_C
            moves.append((d * N_GRP + g, there * N_GRP + line % N_GRP))
    return moves


def halo(north, south):
    above = lax.ppermute(south, ("slide", "grp"), line_moves(1))
    below = lax.ppermute(north, ("slide", "grp"), line_moves(-1))
    return above, below


PLANE = [[z * 8 + k for k in range(8)] for z in range(8)]


def exchange(pieces, groups):
    return lax.all_to_all(
        pieces, "slide", split_axis=0, concat_axis=0, axis_index_groups=groups, tiled=False
    )


def shards(
    features,
    tissue,
    group_owner,
    reduce_weight,
    spatial_weight,
    expand_weight,
    reduce_scale,
    reduce_shift,
    spatial_scale,
    spatial_shift,
    expand_scale,
    expand_shift,
    upstream,
):
    me = jnp.stack([lax.axis_index("grp"), lax.axis_index("slide")]).astype(jnp.int32)
    own = (MID, OWN)
    long = (MID + PARAM_ROWS, OWN)
    side = (16, MID)
    edge = [((MID + 16, WIDE), BF16)] * 2
    half = spatial_weight.shape[1] // 2
    quarter = lax.dynamic_slice_in_dim(spatial_weight, lax.axis_index("slide") % 2 * half, half, 1)
    quarters = [quarter] + [along_grp(quarter, k) for k in (1, 2, 3)]
    strips = call(strip_kernel, [((64, CH), BF16)] * 2, features, upstream, tissue, flops=4 * WIDE * CH * CELLS)
    east, west = beside(strips[0], -1), beside(strips[1], 1)
    mine, = call(weights_kernel, [((N_GRP,) + quarter.shape, BF16)], me, *quarters, smem=(0,), after=(east, west))
    other = pair_swap(mine)
    scales = jnp.stack([reduce_scale, reduce_shift, spatial_scale, spatial_shift])
    with jax.named_scope("reduce"):
        p = call(
            reduce_kernel,
            [(long, BF16)] * 4,
            me, features, reduce_weight, scales, west, east,
            smem=(0,), flops=2 * MID * CH * CELLS, after=(mine,),
        )
        p = [p[0]] + [along_grp(p[k], k) for k in (1, 2, 3)]
    with jax.named_scope("first"):
        first, slope_one, cols, rows, side_one, side_mask, *edges = call(
            first_kernel,
            [(own, BF16), (own, F32), ((MID, WIDE), F32), ((8, MID), F32), (side, BF16), (side, F32)] + edge,
            me, *p, tissue, west, east,
            smem=(0,), flops=40 * MID * OWN, after=(other,),
        )
        edges = halo(*edges)
    with jax.named_scope("second"):
        second, slope_two, side_slope, win = call(
            second_kernel,
            [(long, BF16), (own, F32), (side, F32), ((3, MID, OWN + 2 * WIDE), BF16)],
            me, first, side_one, *edges, mine, other, cols, rows, side_mask, tissue,
            smem=(0,), flops=18 * MID * MID * OWN, scratch=[pltpu.VMEM(own, F32)],
        )
        s = [second] + [along_grp(second, k) for k in (1, 2, 3)]
    with jax.named_scope("expand"):
        output, err, b0, b1, b2, b3, expand_part = call(
            expand_kernel,
            [((CH, CELLS), BF16), ((CH, CELLS), BF16)] + [(long, BF16)] * 4 + [((8, MAT_ROWS, WIDE), BF16)],
            me, *s, expand_weight, features, upstream, expand_scale.reshape(1, -1), expand_shift.reshape(1, -1), tissue, west, east,
            smem=(0,), flops=6 * CH * MID * CELLS,
            scratch=[pltpu.VMEM(own, F32), pltpu.VMEM(own, BF16)],
        )
        b = [b0] + [along_grp(v, -k) for k, v in ((1, b1), (2, b2), (3, b3))]
    with jax.named_scope("merge"):
        packed, = call(
            pack_kernel, [((4 * CH, 4 * CH), BF16)], group_owner.reshape(1, -1), output,
            flops=8 * CH * 4 * CH * OWN,
        )
    with jax.named_scope("back_second"):
        back_two, side_two, *edges = call(
            back_second_kernel,
            [(own, BF16), (side, BF16)] + edge,
            *b, slope_two, side_slope, flops=10 * MID * OWN, after=(packed,),
        )
        edges = halo(*edges)
    with jax.named_scope("spatial"):
        half = (4, N_GRP * SP_ROWS + MAT_ROWS, WIDE)
        keep, send = call(
            spatial_kernel, [(half, BF16)] * 2, me, back_two, win, expand_part,
            smem=(0,), flops=18 * MID * MID * OWN,
        )
        y = call(pair_sum_kernel, [(half[1:], BF16)] * 4, me, keep, pair_swap(send), smem=(0,))
    with jax.named_scope("merge"):
        packed = gate(packed, *edges, y[0])
        arrived = lax.all_to_all(
            packed.reshape(N_SLIDE, 16, 4 * CH), "slide", split_axis=0, concat_axis=0, tiled=False
        ).reshape(4 * CH, 4 * CH)
    with jax.named_scope("back_first"):
        back_one, = call(
            back_first_kernel,
            [(own, BF16)],
            me, back_two, side_two, *edges, mine, other, slope_one,
            smem=(0,), flops=18 * MID * MID * OWN,
            scratch=[pltpu.VMEM((3, MID, OWN + 2 * WIDE), BF16), pltpu.VMEM(own, F32)],
        )
        o = [back_one] + [along_grp(back_one, k) for k in (1, 2, 3)]
    with jax.named_scope("spatial"):
        y = [y[0]] + [along_row(y[k], k) for k in (1, 2, 3)]
        *x, expand_part = call(
            row_sum_kernel, [((SP_ROWS, WIDE), BF16)] * 4 + [((MAT_ROWS, WIDE), BF16)],
            me, *y, smem=(0,),
        )
    with jax.named_scope("early"):
        x = [x[0]] + [along_grp(x[k], k) for k in (1, 2, 3)]
    with jax.named_scope("last"):
        feature_grad, reduce_part, send = call(
            last_kernel,
            [((CH, CELLS), BF16), ((8, MAT_ROWS, WIDE), BF16), ((4, MAT_ROWS, WIDE), BF16)],
            me, *o, reduce_weight, features, err,
            smem=(0,), flops=4 * CH * MID * CELLS,
        )
    with jax.named_scope("merge"):
        merged, = call(
            unpack_kernel, [((4 * CH, 4 * CH), BF16)], arrived,
            flops=4 * 512 * 512 * 4 * CH,
        )
    with jax.named_scope("grads"):
        y = call(
            pair_matrix_kernel, [((MAT_ROWS, WIDE), BF16)] * 4, me, reduce_part, pair_swap(send), smem=(0,)
        )
        y = [y[0]] + [along_row(y[k], k) for k in (1, 2, 3)]
        spread = ((8, SP_ROWS + 2 * MAT_ROWS, WIDE), BF16)
        plane, = call(plane_sum_kernel, [(spread[0][1:], BF16)], *x, expand_part, *y)
        plane, = call(two_sum_kernel, [(spread[0][1:], BF16)], plane, column_swap(plane))
        total, = call(all_sum_kernel, [spread], plane, *[along_column(plane, k) for k in (2, 4, 6)], after=(arrived,))
        reduce_grad, spatial_grad, expand_grad = call(
            finish_kernel,
            [((MID, CH), F32), ((9 * 64, MID), F32), ((CH, MID), F32)],
            exchange(total, PLANE),
        )
    return merged, feature_grad, reduce_grad, spatial_grad.reshape(9, 64, MID), expand_grad


def solution(mesh):
    return jax.shard_map(
        shards,
        mesh=mesh,
        in_specs=(
            P("grp", "slide"),
            P("slide", None),
            P("slide", None),
            P(None, "grp"),
            P(None, "grp", None),
            P("grp", None),
            P("grp"),
            P("grp"),
            P("grp"),
            P("grp"),
            P("grp"),
            P("grp"),
            P("grp", "slide"),
        ),
        out_specs=(
            P("grp", "slide"),
            P("grp", "slide"),
            P(None, "grp"),
            P(None, "grp", None),
            P("grp", None),
        ),
        check_vma=False,
    )
```

```python
import functools
import math

import jax
import jax.numpy as jnp
from jax import lax
from jax.experimental import pallas as pl
from jax.experimental.pallas import tpu as pltpu
from jax.sharding import PartitionSpec as P

F32 = jnp.float32
BF16 = jnp.bfloat16
KAPPA = math.sqrt(2.0 / math.pi)
CUBIC = 0.044715
VMEM_BYTES = 48 * 1024 * 1024

GRID_R = 8
GRID_C = 8
N_SLIDE = 64
N_GRP = 4
TILE_COLS = 32
WIDE = 128
ROWS = 4
OWN = ROWS * WIDE
CELLS = N_GRP * OWN
CH = 256
MID = 256
PARAM_ROWS = 16
TAPS = tuple((a, b) for a in (-1, 0, 1) for b in (-1, 0, 1))
GRAD_SCALE = 1.0 / math.sqrt(N_SLIDE * CELLS)
SP_ROWS = 144
MAT_ROWS = 64


def call(body, outs, *args, flops=0, scratch=(), smem=(), after=()):
    spec = pl.BlockSpec()
    scalar = pl.BlockSpec(memory_space=pltpu.SMEM)
    moved = sum(math.prod(s) * jnp.dtype(d).itemsize for s, d in outs)
    moved += sum(math.prod(a.shape) * a.dtype.itemsize for a in args)
    held = len(args)

    def ordered(*refs):
        body(*refs[:held], *refs[held + len(after) :])

    return pl.pallas_call(
        ordered,
        out_shape=[jax.ShapeDtypeStruct(s, d) for s, d in outs],
        in_specs=[scalar if i in smem else spec for i in range(held)]
        + [pl.BlockSpec(memory_space=pl.ANY)] * len(after),
        out_specs=[spec] * len(outs),
        scratch_shapes=list(scratch),
        compiler_params=pltpu.CompilerParams(vmem_limit_bytes=VMEM_BYTES),
        cost_estimate=pl.CostEstimate(flops=flops, bytes_accessed=moved, transcendentals=0),
    )(*args, *after)


def gate(array, *after):
    place = pl.BlockSpec(memory_space=pl.ANY)
    return pl.pallas_call(
        lambda *refs: None,
        out_shape=jax.ShapeDtypeStruct(array.shape, array.dtype),
        in_specs=[place] * (1 + len(after)),
        out_specs=place,
        input_output_aliases={0: 0},
    )(array, *after)


def dot(lhs, rhs, left=1, right=0):
    return lax.dot_general(lhs, rhs, (((left,), (right,)), ((), ())), preferred_element_type=F32)


def act_parts(v):
    sq = v * v
    t = jnp.tanh(v * (KAPPA + (KAPPA * CUBIC) * sq))
    half = 0.5 + 0.5 * t
    value = v * half
    slope = half + (value * (1.0 - t)) * (KAPPA + (3.0 * KAPPA * CUBIC) * sq)
    return value, slope


def tile_mask(tissue_row):
    spread = (
        lax.broadcasted_iota(jnp.int32, (TILE_COLS, WIDE), 1) // 4
        == lax.broadcasted_iota(jnp.int32, (TILE_COLS, WIDE), 0)
    ).astype(F32)
    row = tissue_row.astype(F32)
    if row.shape[0] == 1:
        row = jnp.broadcast_to(row, (8, TILE_COLS))
    return dot(row, spread)[:1]


def lanes(shape):
    return lax.broadcasted_iota(jnp.int32, shape, len(shape) - 1)


def side_flags(me):
    col = me[1] % GRID_C
    return (col > 0).astype(F32), (col < GRID_C - 1).astype(F32)


def strip_kernel(feat, ups, tissue, left_out, right_out):
    place = lax.broadcasted_iota(jnp.int32, (WIDE, CELLS), 0)
    cell = lanes((WIDE, CELLS))
    kind, row = place % 64 // 16, place % 16
    col = jnp.where(place < 64, kind, WIDE - 1 - kind)
    edge = jnp.where(place < 64, 0, WIDE - 1)
    here = cell // WIDE == row
    pick = (here & (cell % WIDE == col) & (kind < 2)).astype(F32).astype(BF16)
    pick_ups = (here & (cell % WIDE == edge) & (kind == 2)).astype(F32).astype(BF16)
    strips = dot(pick, feat[...], 1, 1) + dot(pick_ups, ups[...], 1, 1)
    tiles = tissue[...].astype(F32)
    for out, lo, at in ((left_out, 0, 0), (right_out, 64, TILE_COLS - 1)):
        out[:48] = strips[lo : lo + 48].astype(BF16)
        flags = [jnp.broadcast_to(tiles[q : q + 1, at : at + 1], (4, CH)) for q in range(N_GRP)]
        out[48:] = jnp.concatenate(flags, 0).astype(BF16)


def reduce_kernel(me, feat, weight, scales, west, east, *outs):
    g = me[0]
    par = jnp.concatenate([scales[...]] * N_GRP, 1)
    par = jnp.where(lanes((4, MID)) // (MID // N_GRP) == g, par, 0.0)
    hi = par.astype(BF16)
    rest = par - hi.astype(F32)
    mid = rest.astype(BF16)
    low = (rest - mid.astype(F32)).astype(BF16)
    tail = jnp.concatenate(
        [hi.astype(F32), mid.astype(F32), low.astype(F32), jnp.zeros((4, MID), F32)], 0
    ).astype(BF16)
    sides = dot(jnp.concatenate([west[:32], east[:32]], 0), weight[...], 1, 1)
    for k in range(N_GRP):
        q = (g + k) % N_GRP
        start = pl.multiple_of(q * OWN, OWN)
        block = dot(weight[...], feat[:, pl.ds(start, OWN)])
        outs[k][:MID] = block.astype(BF16)
        outs[k][MID:, :MID] = tail
        mine = pick_rows(sides, q, 4)
        outs[k][MID:, MID:] = mine.astype(BF16)


def pick_rows(cells, q, groups):
    picked = []
    for n in range(groups):
        rows = jnp.zeros((4, cells.shape[1]), F32)
        for j in range(N_GRP):
            rows = jnp.where(q == j, cells[n * 16 + 4 * j : n * 16 + 4 * j + 4], rows)
        picked.append(rows)
    return jnp.concatenate(picked, 0)


def weights_kernel(me, w0, w1, w2, w3, out):
    for k, w in enumerate((w0, w1, w2, w3)):
        out[(me[0] + N_GRP - k) % N_GRP] = w[...]


def tap_weight(me, mine, other, t):
    core = me[1] % 2
    rows = []
    for q in range(N_GRP):
        here, there = mine[q, t], other[q, t]
        rows += [jnp.where(core == 0, here, there), jnp.where(core == 0, there, here)]
    return jnp.concatenate(rows, 0)


def first_kernel(
    me, p0, p1, p2, p3, tissue, west, east,
    act_out, slope_out, cols_out, rows_out, side_out, side_mask, north_out, south_out,
):
    g = me[0]
    tails = [p[MID:].astype(F32) for p in (p0, p1, p2, p3)]
    rows = (tails[0] + tails[1]) + (tails[2] + tails[3])
    par = (rows[0:4, :MID] + rows[4:8, :MID]) + rows[8:12, :MID]
    rows_out[...] = jnp.concatenate([par, jnp.zeros((4, MID), F32)], 0)
    cols = jnp.concatenate([par, jnp.zeros((124, MID), F32)], 0).T
    cols_out[...] = cols
    lhs, rhs = side_flags(me)
    west_mask = pick_rows(west[48:].astype(F32), g, 1) * lhs
    east_mask = pick_rows(east[48:].astype(F32), g, 1) * rhs
    flags = jnp.concatenate([west_mask, west_mask, east_mask, east_mask], 0)
    side_mask[...] = flags
    side, _ = act_parts(par[0:1] * rows[:, MID:] + par[1:2])
    side_out[...] = (flags * side).astype(BF16)
    mask = tile_mask(tissue[pl.ds(g, 1), :])
    for lo in range(0, MID, 32):
        part = slice(lo, lo + 32)
        scale = cols[part, 0:1]
        shift = cols[part, 1:2]
        for r in range(ROWS):
            seg = slice(r * WIDE, (r + 1) * WIDE)
            total = (p0[part, seg].astype(F32) + p1[part, seg].astype(F32)) + (
                p2[part, seg].astype(F32) + p3[part, seg].astype(F32)
            )
            value, slope = act_parts(scale * total + shift)
            act_out[part, seg] = (mask * value).astype(BF16)
            slope_out[part, seg] = (scale * mask) * slope
    put_edges(act_out, side_out, north_out, south_out)


def put_edges(grid, side, north_out, south_out):
    cells = side[...].astype(F32)
    for out, r in ((north_out, 0), (south_out, ROWS - 1)):
        out[:MID] = grid[:, r * WIDE : (r + 1) * WIDE]
        lines = []
        for n in range(4):
            cell = cells[4 * n + r : 4 * n + r + 1]
            lines += [cell[:, :WIDE], cell[:, WIDE:]]
        out[MID:] = jnp.concatenate(lines + [jnp.zeros((8, WIDE), F32)], 0).astype(BF16)


def side_rows(me, side, above, below):
    g, s = me[0], me[1]
    north = ((g > 0) | (s >= GRID_C)).astype(F32)
    south = ((g < N_GRP - 1) | (s < N_SLIDE - GRID_C)).astype(F32)
    cells = side[...].astype(F32)
    up = above[MID:].astype(F32) * north
    down = below[MID:].astype(F32) * south
    kinds = []
    for n in range(4):
        first = jnp.concatenate([up[2 * n : 2 * n + 1], up[2 * n + 1 : 2 * n + 2]], 1)
        last = jnp.concatenate([down[2 * n : 2 * n + 1], down[2 * n + 1 : 2 * n + 2]], 1)
        kinds.append(jnp.concatenate([first, cells[4 * n : 4 * n + 4], last], 0))
    return north, south, kinds


def shifted(me, grid, side, above, below, out):
    north, south, kinds = side_rows(me, side, above, below)
    columns = jnp.concatenate(
        [kinds[0], kinds[2], jnp.zeros((WIDE - 2 * (ROWS + 2), MID), F32)], 0
    ).T
    lane = lanes((MID, WIDE))
    for r in range(ROWS + 2):
        seg = slice(r * WIDE, (r + 1) * WIDE)
        if r == 0:
            row = above[:MID].astype(F32) * north
        elif r == ROWS + 1:
            row = below[:MID].astype(F32) * south
        else:
            row = grid[:, (r - 1) * WIDE : r * WIDE].astype(F32)
        lcol = columns[:, r : r + 1]
        rcol = columns[:, ROWS + 2 + r : ROWS + 3 + r]
        out[1, :, seg] = row.astype(BF16)
        out[0, :, seg] = jnp.where(lane == 0, lcol, pltpu.roll(row, 1, 1)).astype(BF16)
        out[2, :, seg] = jnp.where(lane == WIDE - 1, rcol, pltpu.roll(row, WIDE - 1, 1)).astype(BF16)
    return kinds


def second_kernel(
    me, grid, side, above, below, mine, other, cols, rows, side_mask, tissue,
    act_out, slope_out, side_slope, win_out, acc,
):
    near_west, next_west, near_east, next_east = shifted(me, grid, side, above, below, win_out)
    ends = (
        lanes((16, WIDE)) == (WIDE - 1) * (lax.broadcasted_iota(jnp.int32, (16, WIDE), 0) // 8)
    ).astype(F32).astype(BF16)
    firsts, lasts = [], []
    for r in range(ROWS + 2):
        both = dot(ends, win_out[1, :, r * WIDE : (r + 1) * WIDE], 1, 1)
        firsts.append(both[0:1])
        lasts.append(both[8:9])
    first_col = jnp.concatenate(firsts, 0)
    last_col = jnp.concatenate(lasts, 0)
    blank = jnp.zeros((4, MID), F32)
    side_acc = jnp.zeros((16, MID), F32)
    for t, (a, b) in enumerate(TAPS):
        w = tap_weight(me, mine, other, t)
        start = (a + 1) * WIDE
        part = dot(w, win_out[b + 1, :, start : start + OWN])
        acc[...] = part if t == 0 else acc[...] + part
        lhs = (next_west, near_west, first_col)[b + 1][a + 1 : a + 5]
        rhs = (last_col, near_east, next_east)[b + 1][a + 1 : a + 5]
        patch = jnp.concatenate([lhs, blank, rhs, blank], 0).astype(BF16)
        side_acc = side_acc + dot(patch, w, 1, 1)
    scale_row, shift_row = rows[2:3], rows[3:4]
    value, slope = act_parts(scale_row * side_acc + shift_row)
    act_out[MID:, :MID] = (side_mask[...] * value).astype(BF16)
    act_out[MID:, MID:] = jnp.zeros((16, OWN - MID), BF16)
    side_slope[...] = (scale_row * side_mask[...]) * slope
    mask = tile_mask(tissue[pl.ds(me[0], 1), :])
    for lo in range(0, MID, 32):
        part = slice(lo, lo + 32)
        scale = cols[part, 2:3]
        shift = cols[part, 3:4]
        for r in range(ROWS):
            seg = slice(r * WIDE, (r + 1) * WIDE)
            value, slope = act_parts(scale * acc[part, seg] + shift)
            act_out[part, seg] = (mask * value).astype(BF16)
            slope_out[part, seg] = (scale * mask) * slope


def expand_kernel(me, s0, s1, s3, s2, weight, feat, ups, scales, shifts, tissue, west, east, out, err_out, b0, b1, b2, b3, grad_out, acc, back):
    g = me[0]
    par = jnp.concatenate([scales[...], shifts[...], jnp.zeros((126, CH), F32)], 0).T
    cells = [jnp.zeros((16, MID), F32)] * 2
    group = lax.broadcasted_iota(jnp.int32, (16, MID), 0) // 4
    for k, s in enumerate((s0, s1, s2, s3)):
        q = (g + N_GRP - k) % N_GRP
        tail = s[MID:, :MID].astype(F32)
        for n in range(2):
            cells[n] = jnp.where(group == q, jnp.concatenate([tail[8 * n : 8 * n + 4]] * 4, 0), cells[n])
    scale_row, shift_row = scales[...], shifts[...]
    wide = dot(jnp.concatenate(cells, 0).astype(BF16), weight[...], 1, 1)
    errs = []
    for n, (strip, flag) in enumerate(zip((west, east), side_flags(me))):
        pre = strip[:16].astype(F32) + scale_row * wide[16 * n : 16 * n + 16] + shift_row
        _, slope = act_parts(pre)
        errs.append(scale_row * (slope * (strip[48:].astype(F32) * flag) * strip[32:48].astype(F32)))
    sides = dot(jnp.concatenate(errs, 0).astype(BF16), weight[...])
    blank = jnp.zeros((4, MID), F32)
    grad = None
    for k, (s, b_out) in enumerate(((s0, b0), (s1, b1), (s2, b2), (s3, b3))):
        q = (g + N_GRP - k) % N_GRP
        base = pl.multiple_of(q * OWN, OWN)
        acc[...] = dot(weight[...], s[:MID])
        mine = pick_rows(sides, q, 2)
        b_out[MID:, :MID] = jnp.concatenate([mine[:4], blank, mine[4:], blank], 0).astype(BF16)
        b_out[MID:, MID:] = jnp.zeros((16, OWN - MID), BF16)
        mask = tile_mask(tissue[pl.ds(q, 1), :])
        for lo in range(0, CH, 32):
            part = slice(lo, lo + 32)
            scale = par[part, 0:1]
            shift = par[part, 1:2]
            for r in range(ROWS):
                seg = pl.ds(pl.multiple_of(base + r * WIDE, WIDE), WIDE)
                here = slice(r * WIDE, (r + 1) * WIDE)
                pre = feat[part, seg].astype(F32) + scale * acc[part, here] + shift
                value, slope = act_parts(pre)
                err = slope * (mask * ups[part, seg].astype(F32))
                out[part, seg] = (mask * value).astype(BF16)
                err_out[part, seg] = err.astype(BF16)
                back[part, here] = (scale * err).astype(BF16)
        b_out[:MID] = dot(weight[...], back[...], 0, 0).astype(BF16)
        term = dot(back[...], s[:MID], 1, 1)
        grad = term if grad is None else grad + term
    put_matrix(grad_out, grad)


def put_matrix(out, matrix):
    for p in range(8):
        q, h = divmod(p, 2)
        out[p] = matrix[q * MAT_ROWS : (q + 1) * MAT_ROWS, h * WIDE : (h + 1) * WIDE].astype(BF16)


def pack_kernel(owner, out, packed):
    row_own = jnp.broadcast_to(owner[...], (WIDE, WIDE))
    sub = lax.broadcasted_iota(jnp.int32, (WIDE, WIDE), 0)
    lane = lanes((WIDE, WIDE))
    col_own = jnp.sum(jnp.where(sub == lane, row_own, 0), 1, keepdims=True)
    rank = jnp.sum(jnp.where((col_own == row_own) & (lane < sub), 1, 0), 1, keepdims=True)
    slot = jnp.broadcast_to(col_own * 4 + rank, (WIDE, WIDE))
    pick = lane % 64
    cell = 4 * (pick // 2) + 2 * (pick % 2)
    even = (sub == cell + lane // 64).astype(BF16)
    odd = (sub == cell + 1 - lane // 64).astype(BF16)
    target = []
    for x in range(N_GRP):
        mine = jnp.where(sub == x * TILE_COLS + pick // 2, slot, 0)
        spot = jnp.sum(mine, 0, keepdims=True) * 4 + pick[:1] % 2
        target.append(spot)
    upper = lanes((1, WIDE)) // 64
    low = lanes((CH, WIDE)) < 64
    for j in range(2):
        goal = jnp.concatenate([t + 2 * ((upper + j) % 2) for t in target], 1)
        column = lax.broadcasted_iota(jnp.int32, (4 * CH, OWN), 0)
        select = (column == goal).astype(F32).astype(BF16)
        for i in range(2):
            pieces = []
            for x in range(N_GRP):
                at = x * OWN + i * WIDE
                first = dot(out[:, at : at + WIDE], even)
                second = dot(out[:, at + 2 * WIDE : at + 3 * WIDE], odd)
                if j == 0:
                    pieces.append(jnp.where(low, first, second).astype(BF16))
                else:
                    pieces.append(jnp.where(low, second, first).astype(BF16))
            moved = dot(select, jnp.concatenate(pieces, 1), 1, 1).astype(BF16)
            ij = 2 * i + j
            for h in range(2):
                packed[:, h * 512 + ij * WIDE : h * 512 + (ij + 1) * WIDE] = moved[:, h * WIDE : (h + 1) * WIDE]


def unpack_kernel(packed, out):
    row = lax.broadcasted_iota(jnp.int32, (512, 512), 0)
    col = lanes((512, 512))
    order = (col == (row % 4) * WIDE + row // 4).astype(F32).astype(BF16)
    for h in range(2):
        part = slice(h * 512, (h + 1) * 512)
        out[part] = dot(order, packed[:, part], 1, 1).astype(BF16)


def back_second_kernel(b0, b1, b2, b3, slope, side_slope, grid_out, side_out, north_out, south_out):
    tails = [b[MID:, :MID].astype(F32) for b in (b0, b1, b2, b3)]
    side_out[...] = (side_slope[...] * ((tails[0] + tails[1]) + (tails[2] + tails[3]))).astype(BF16)
    for lo in range(0, MID, 32):
        part = slice(lo, lo + 32)
        total = (b0[part].astype(F32) + b1[part].astype(F32)) + (b2[part].astype(F32) + b3[part].astype(F32))
        grid_out[part] = (slope[part] * total).astype(BF16)
    put_edges(grid_out, side_out, north_out, south_out)


def back_first_kernel(me, grid, side, above, below, mine, other, slope, back_out, win, acc):
    shifted(me, grid, side, above, below, win)
    for t, (a, b) in enumerate(TAPS):
        w = tap_weight(me, mine, other, t)
        start = (1 - a) * WIDE
        part = dot(w, win[1 - b, :, start : start + OWN], 0, 0)
        acc[...] = part if t == 0 else acc[...] + part
    back_out[...] = (slope[...] * acc[...]).astype(BF16)


def spatial_kernel(me, grid, win, expand_part, keep, send):
    core = me[1] % 2
    for t, (a, b) in enumerate(TAPS):
        start = (a + 1) * WIDE
        term = dot(grid[...], win[b + 1, :, start : start + OWN], 1, 1)
        lo, hi = term[:, :WIDE], term[:, WIDE:]
        mine = jnp.where(core == 0, lo, hi).astype(BF16)
        other = jnp.where(core == 0, hi, lo).astype(BF16)
        for q in range(N_GRP):
            for at in range(0, 64, 16):
                block, within = divmod(t * 64 + at, SP_ROWS)
                rows = slice(q * SP_ROWS + within, q * SP_ROWS + within + 16)
                keep[block, rows] = mine[q * 64 + at : q * 64 + at + 16]
                send[block, rows] = other[q * 64 + at : q * 64 + at + 16]
    for block in range(4):
        keep[block, N_GRP * SP_ROWS :] = expand_part[2 * block + core]
        send[block, N_GRP * SP_ROWS :] = expand_part[2 * block + 1 - core]


def pair_sum_kernel(me, keep, got, y0, y1, y2, y3):
    row = me[1] // 2 % 4
    for k, out in enumerate((y0, y1, y2, y3)):
        q = (row + k) % 4
        out[...] = (keep[q].astype(F32) + got[q].astype(F32)).astype(BF16)


def row_sum_kernel(me, y0, y1, y2, y3, x0, x1, x2, x3, matrix):
    def total(rows):
        return (
            (y0[rows].astype(F32) + y1[rows].astype(F32)) + (y2[rows].astype(F32) + y3[rows].astype(F32))
        ).astype(BF16)

    for k, out in enumerate((x0, x1, x2, x3)):
        start = pl.multiple_of(((me[0] + k) % N_GRP) * SP_ROWS, 16)
        out[...] = total(pl.ds(start, SP_ROWS))
    matrix[...] = total(slice(N_GRP * SP_ROWS, N_GRP * SP_ROWS + MAT_ROWS))


def last_kernel(me, o0, o1, o3, o2, weight, feat, err, out, grad_out, send):
    g = me[0]
    grad = None
    for k, o in enumerate((o0, o1, o2, o3)):
        base = pl.multiple_of(((g + N_GRP - k) % N_GRP) * OWN, OWN)
        seg = pl.ds(base, OWN)
        out[:, seg] = (err[:, seg].astype(F32) + dot(weight[...], o[...], 0, 0)).astype(BF16)
        term = dot(o[...], feat[:, seg], 1, 1)
        grad = term if grad is None else grad + term
    put_matrix(grad_out, grad)
    core = me[1] % 2
    for q in range(4):
        send[q] = grad_out[2 * q + 1 - core]


def pair_matrix_kernel(me, part, got, y0, y1, y2, y3):
    core = me[1] % 2
    row = me[1] // 2 % 4
    for k, out in enumerate((y0, y1, y2, y3)):
        q = (row + k) % 4
        out[...] = (part[2 * q + core].astype(F32) + got[q].astype(F32)).astype(BF16)


def plane_sum_kernel(x0, x1, x2, x3, expand_part, y0, y1, y2, y3, out):
    spatial = (x0[...].astype(F32) + x1[...].astype(F32)) + (x2[...].astype(F32) + x3[...].astype(F32))
    total = (y0[...].astype(F32) + y1[...].astype(F32)) + (y2[...].astype(F32) + y3[...].astype(F32))
    spatial = spatial.astype(BF16)
    total = total.astype(BF16)
    out[:SP_ROWS] = spatial
    out[SP_ROWS : SP_ROWS + MAT_ROWS] = expand_part[...]
    out[SP_ROWS + MAT_ROWS :] = total


def two_sum_kernel(one, two, out):
    out[...] = (one[...].astype(F32) + two[...].astype(F32)).astype(BF16)


def all_sum_kernel(*refs):
    parts, out = refs[:-1], refs[-1]
    total = parts[0][...].astype(F32)
    for part in parts[1:]:
        total = total + part[...].astype(F32)
    total = total.astype(BF16)
    for p in range(8):
        out[p] = total


def finish_kernel(parts, reduce_out, spatial_out, expand_out):
    for p in range(8):
        q, h = divmod(p, 2)
        seg = slice(h * WIDE, (h + 1) * WIDE)
        spatial_out[q * SP_ROWS : (q + 1) * SP_ROWS, seg] = parts[p, :SP_ROWS].astype(F32) * GRAD_SCALE
        rows = slice(q * MAT_ROWS, (q + 1) * MAT_ROWS)
        expand_out[rows, seg] = parts[p, SP_ROWS : SP_ROWS + MAT_ROWS].astype(F32) * GRAD_SCALE
        reduce_out[rows, seg] = parts[p, SP_ROWS + MAT_ROWS :].astype(F32) * GRAD_SCALE


def along_grp(block, step):
    return lax.ppermute(block, "grp", [(i, (i + step) % N_GRP) for i in range(N_GRP)])


def pair_swap(block):
    return lax.ppermute(block, "slide", [(d, d ^ 1) for d in range(N_SLIDE)])


def along_row(block, step):
    moves = [(d, d // 8 * 8 + (d + 2 * step) % 8) for d in range(N_SLIDE)]
    return lax.ppermute(block, "slide", moves)


def column_swap(block):
    return lax.ppermute(block, "slide", [(d, d ^ 8) for d in range(N_SLIDE)])


def along_column(block, step):
    return lax.ppermute(block, "slide", [(d, (d + 8 * step) % N_SLIDE) for d in range(N_SLIDE)])


def beside(block, step):
    moves = [(d, d // GRID_C * GRID_C + (d + step) % GRID_C) for d in range(N_SLIDE)]
    return lax.ppermute(block, "slide", moves)


def line_moves(step):
    moves = []
    for d in range(N_SLIDE):
        for g in range(N_GRP):
            line = (d // GRID_C * N_GRP + g + step) % (GRID_R * N_GRP)
            there = line // N_GRP * GRID_C + d % GRID_C
            moves.append((d * N_GRP + g, there * N_GRP + line % N_GRP))
    return moves


def halo(north, south):
    above = lax.ppermute(south, ("slide", "grp"), line_moves(1))
    below = lax.ppermute(north, ("slide", "grp"), line_moves(-1))
    return above, below


PLANE = [[z * 8 + k for k in range(8)] for z in range(8)]


def exchange(pieces, groups):
    return lax.all_to_all(
        pieces, "slide", split_axis=0, concat_axis=0, axis_index_groups=groups, tiled=False
    )


def shards(
    features,
    tissue,
    group_owner,
    reduce_weight,
    spatial_weight,
    expand_weight,
    reduce_scale,
    reduce_shift,
    spatial_scale,
    spatial_shift,
    expand_scale,
    expand_shift,
    upstream,
):
    me = jnp.stack([lax.axis_index("grp"), lax.axis_index("slide")]).astype(jnp.int32)
    own = (MID, OWN)
    long = (MID + PARAM_ROWS, OWN)
    side = (16, MID)
    edge = [((MID + 16, WIDE), BF16)] * 2
    half = spatial_weight.shape[1] // 2
    quarter = lax.dynamic_slice_in_dim(spatial_weight, lax.axis_index("slide") % 2 * half, half, 1)
    quarters = [quarter] + [along_grp(quarter, k) for k in (1, 2, 3)]
    strips = call(strip_kernel, [((64, CH), BF16)] * 2, features, upstream, tissue, flops=4 * WIDE * CH * CELLS)
    east, west = beside(strips[0], -1), beside(strips[1], 1)
    mine, = call(weights_kernel, [((N_GRP,) + quarter.shape, BF16)], me, *quarters, smem=(0,), after=(east, west))
    other = pair_swap(mine)
    scales = jnp.stack([reduce_scale, reduce_shift, spatial_scale, spatial_shift])
    with jax.named_scope("reduce"):
        p = call(
            reduce_kernel,
            [(long, BF16)] * 4,
            me, features, reduce_weight, scales, west, east,
            smem=(0,), flops=2 * MID * CH * CELLS, after=(mine,),
        )
        p = [p[0]] + [along_grp(p[k], k) for k in (2, 1, 3)]
    with jax.named_scope("first"):
        first, slope_one, cols, rows, side_one, side_mask, *edges = call(
            first_kernel,
            [(own, BF16), (own, F32), ((MID, WIDE), F32), ((8, MID), F32), (side, BF16), (side, F32)] + edge,
            me, *p, tissue, west, east,
            smem=(0,), flops=40 * MID * OWN, after=(other,),
        )
        edges = halo(*edges)
    with jax.named_scope("second"):
        second, slope_two, side_slope, win = call(
            second_kernel,
            [(long, BF16), (own, F32), (side, F32), ((3, MID, OWN + 2 * WIDE), BF16)],
            me, first, side_one, *edges, mine, other, cols, rows, side_mask, tissue,
            smem=(0,), flops=18 * MID * MID * OWN, scratch=[pltpu.VMEM(own, F32)],
        )
        s = [second] + [along_grp(second, k) for k in (1, 3, 2)]
    with jax.named_scope("expand"):
        output, err, b0, b1, b2, b3, expand_part = call(
            expand_kernel,
            [((CH, CELLS), BF16), ((CH, CELLS), BF16)] + [(long, BF16)] * 4 + [((8, MAT_ROWS, WIDE), BF16)],
            me, *s, expand_weight, features, upstream, expand_scale.reshape(1, -1), expand_shift.reshape(1, -1), tissue, west, east,
            smem=(0,), flops=6 * CH * MID * CELLS,
            scratch=[pltpu.VMEM(own, F32), pltpu.VMEM(own, BF16)],
        )
        b = [b0] + [along_grp(v, -k) for k, v in ((2, b2), (1, b1), (3, b3))]
    with jax.named_scope("merge"):
        packed, = call(
            pack_kernel, [((4 * CH, 4 * CH), BF16)], group_owner.reshape(1, -1), output,
            flops=8 * CH * 4 * CH * OWN,
        )
    with jax.named_scope("back_second"):
        back_two, side_two, *edges = call(
            back_second_kernel,
            [(own, BF16), (side, BF16)] + edge,
            *b, slope_two, side_slope, flops=10 * MID * OWN, after=(packed,),
        )
        edges = halo(*edges)
    with jax.named_scope("spatial"):
        half = (4, N_GRP * SP_ROWS + MAT_ROWS, WIDE)
        keep, send = call(
            spatial_kernel, [(half, BF16)] * 2, me, back_two, win, expand_part,
            smem=(0,), flops=18 * MID * MID * OWN,
        )
        y = call(pair_sum_kernel, [(half[1:], BF16)] * 4, me, keep, pair_swap(send), smem=(0,))
    with jax.named_scope("merge"):
        packed = gate(packed, *edges, y[0])
        arrived = lax.all_to_all(
            packed.reshape(N_SLIDE, 16, 4 * CH), "slide", split_axis=0, concat_axis=0, tiled=False
        ).reshape(4 * CH, 4 * CH)
    with jax.named_scope("back_first"):
        back_one, = call(
            back_first_kernel,
            [(own, BF16)],
            me, back_two, side_two, *edges, mine, other, slope_one,
            smem=(0,), flops=18 * MID * MID * OWN,
            scratch=[pltpu.VMEM((3, MID, OWN + 2 * WIDE), BF16), pltpu.VMEM(own, F32)],
        )
        o = [back_one] + [along_grp(back_one, k) for k in (1, 3, 2)]
    with jax.named_scope("spatial"):
        y = [y[0]] + [along_row(y[k], k) for k in (1, 2, 3)]
        *x, expand_part = call(
            row_sum_kernel, [((SP_ROWS, WIDE), BF16)] * 4 + [((MAT_ROWS, WIDE), BF16)],
            me, *y, smem=(0,),
        )
    with jax.named_scope("early"):
        x = [x[0]] + [along_grp(x[k], k) for k in (1, 2, 3)]
    with jax.named_scope("last"):
        feature_grad, reduce_part, send = call(
            last_kernel,
            [((CH, CELLS), BF16), ((8, MAT_ROWS, WIDE), BF16), ((4, MAT_ROWS, WIDE), BF16)],
            me, *o, reduce_weight, features, err,
            smem=(0,), flops=4 * CH * MID * CELLS,
        )
    with jax.named_scope("merge"):
        merged, = call(
            unpack_kernel, [((4 * CH, 4 * CH), BF16)], arrived,
            flops=4 * 512 * 512 * 4 * CH,
        )
    with jax.named_scope("grads"):
        y = call(
            pair_matrix_kernel, [((MAT_ROWS, WIDE), BF16)] * 4, me, reduce_part, pair_swap(send), smem=(0,)
        )
        y = [y[0]] + [along_row(y[k], k) for k in (1, 2, 3)]
        spread = ((8, SP_ROWS + 2 * MAT_ROWS, WIDE), BF16)
        plane, = call(plane_sum_kernel, [(spread[0][1:], BF16)], *x, expand_part, *y)
        plane, = call(two_sum_kernel, [(spread[0][1:], BF16)], plane, column_swap(plane))
        total, = call(all_sum_kernel, [spread], plane, *[along_column(plane, k) for k in (2, 4, 6)], after=(arrived,))
        reduce_grad, spatial_grad, expand_grad = call(
            finish_kernel,
            [((MID, CH), F32), ((9 * 64, MID), F32), ((CH, MID), F32)],
            exchange(total, PLANE),
        )
    return merged, feature_grad, reduce_grad, spatial_grad.reshape(9, 64, MID), expand_grad


def solution(mesh):
    return jax.shard_map(
        shards,
        mesh=mesh,
        in_specs=(
            P("grp", "slide"),
            P("slide", None),
            P("slide", None),
            P(None, "grp"),
            P(None, "grp", None),
            P("grp", None),
            P("grp"),
            P("grp"),
            P("grp"),
            P("grp"),
            P("grp"),
            P("grp"),
            P("grp", "slide"),
        ),
        out_specs=(
            P("grp", "slide"),
            P("grp", "slide"),
            P(None, "grp"),
            P(None, "grp", None),
            P("grp", None),
        ),
        check_vma=False,
    )
```
